32 devices in a mesh: blk: 8 (over y, x, core), uly: 4 (over z).
Axes of the slice: x: 2, y: 2, z: 4, core: 2. Of those that a mesh axis runs over, the one named last changes fastest.
Arguments:
- stored_query_rows: bfloat16 [512, 5120], P('blk', 'uly'), may hold values from -4 to 4
- key_states: bfloat16 [512, 1024], P('blk', 'uly'), may hold values from -4 to 4
- value_states: bfloat16 [512, 1024], P('blk', 'uly'), may hold values from -6 to 6
- attn_output: bfloat16 [512, 5120], P('blk', 'uly'), may hold values from -6 to 6
- output_grad: bfloat16 [512, 5120], P(('blk', 'uly')), may hold values from -48 to 48
- logsumexp: float32 [40, 512], P('uly', 'blk'), may hold values from 7 to 8.5
Outputs:
- query_gradient: bfloat16 [512, 5120], P(('blk', 'uly'))
- key_grad: bfloat16 [512, 1024], P(('blk', 'uly'))
- value_grad: bfloat16 [512, 1024], P(('blk', 'uly'))
The draws below stay inside these ranges and needn't reach their ends.
All inputs are finite; a program needn't handle non-finite values.
Results may differ from the reference program's by a relative error of at most 0.0055.
Values may be sent and summed in bfloat16 or wider, within the bound.
No kernel may reach another device: no remote copies, remote signals or barrier semaphores. Data moves between devices by JAX's collectives and lax.ppermute only.
A program may use at most 64 MiB of HBM per device.

```python
import jax
import jax.numpy as jnp
from jax import lax

QHEADS = 40
KVHEADS = 8
HEAD_DIM = 128
STEPS = 3
BLK = 64
BLOCKS = 8
SEQ = 512


def block_levels(rng, dims, cuts, low, top_value):
    loudness = 1.0
    for position, parts in cuts:
        steps = jax.random.uniform(jax.random.fold_in(jax.random.fold_in(rng, 6), position), (parts,), jnp.float32, low / len(cuts), top_value / len(cuts))
        loudness = loudness * jnp.repeat(jnp.exp(steps), dims[position] // parts).reshape((-1,) + (1,) * (len(dims) - 1 - position))
    return loudness


def gaussian(rng, shape, spread, bound, pieces=(), kind=jnp.bfloat16):
    array = spread * jax.random.normal(rng, shape, jnp.float32)
    if pieces:
        array = array * block_levels(rng, shape, pieces, -0.22, 0.18)
    return jnp.clip(array, -bound, bound).astype(kind)


def setup_inputs(seed: int = 0) -> dict:
    keys = jax.random.split(jax.random.key(seed), 7)
    return {
        "stored_query_rows": gaussian(keys[0], (SEQ, QHEADS * HEAD_DIM), 1.0, 4.0, ((0, 8), (1, 4))),
        "key_states": gaussian(keys[1], (SEQ, KVHEADS * HEAD_DIM), 1.0, 4.0, ((0, 8), (1, 4))),
        "value_states": gaussian(keys[2], (SEQ, KVHEADS * HEAD_DIM), 1.0, 6.0, ((0, 8), (1, 4))),
        "attn_output": gaussian(keys[3], (SEQ, QHEADS * HEAD_DIM), 1.0, 6.0, ((0, 8), (1, 4))),
        "output_grad": gaussian(keys[4], (SEQ, QHEADS * HEAD_DIM), 8.0, 48.0, ((0, 32),)),
        "logsumexp": jnp.clip(7.0 + 1.5 * jax.random.uniform(keys[5], (QHEADS, SEQ), jnp.float32) ** block_levels(keys[5], (QHEADS, SEQ), ((0, 4), (1, 8)), -0.2, 0.2), 7.0, 8.5),
    }


def block_grads(query_heads, gradient_per_head, lse_heads, delta_per_head, key_block, value_block, score_scale):
    query_wide = query_heads.astype(jnp.float32)
    gradient_side_by_side = gradient_per_head.astype(jnp.float32)
    key_wide = key_block.astype(jnp.float32)
    value_wide = value_block.astype(jnp.float32)
    scores = jnp.einsum("tgrd,ugd->grtu", query_wide, key_wide)
    prob_tile = jnp.exp(scores * score_scale - lse_heads[..., None])
    grad_probs = jnp.einsum("tgrd,ugd->grtu", gradient_side_by_side, value_wide)
    grad_scores = (prob_tile * (grad_probs - delta_per_head[..., None])).astype(jnp.bfloat16).astype(jnp.float32)
    prob_low = prob_tile.astype(jnp.bfloat16).astype(jnp.float32)
    value_part = jnp.einsum("grtu,tgrd->ugd", prob_low, gradient_side_by_side)
    query_part = jnp.einsum("grtu,ugd->tgrd", grad_scores, key_wide)
    key_portion = jnp.einsum("grtu,tgrd->ugd", grad_scores, query_wide)
    return query_part, key_portion, value_part


def reference(stored_query_rows, key_states, value_states, attn_output, output_grad, logsumexp):
    group_size = QHEADS // KVHEADS
    score_scale = HEAD_DIM ** -0.5
    query_blocks = stored_query_rows.reshape(BLOCKS, BLK, KVHEADS, group_size, HEAD_DIM)
    grad_blocks = output_grad.reshape(BLOCKS, BLK, KVHEADS, group_size, HEAD_DIM)
    out_blocks = attn_output.reshape(BLOCKS, BLK, KVHEADS, group_size, HEAD_DIM)
    key_blocks = key_states.reshape(BLOCKS, BLK, KVHEADS, HEAD_DIM)
    value_blocks = value_states.reshape(BLOCKS, BLK, KVHEADS, HEAD_DIM)
    lse_blocks = logsumexp.reshape(KVHEADS, group_size, BLOCKS, BLK).transpose(2, 0, 1, 3)

    def one_block(index):
        query_heads = query_blocks[index]
        gradient_per_head = grad_blocks[index]
        output_per_head = out_blocks[index]
        lse_heads = lse_blocks[index]
        delta_per_head = jnp.einsum("lpnc,lpnc->pnl", gradient_per_head.astype(jnp.float32), output_per_head.astype(jnp.float32))
        query_sum = jnp.zeros((BLK, KVHEADS, group_size, HEAD_DIM), jnp.float32)
        key_list = []
        value_list = []
        for offset in range(STEPS):
            source = ((index - offset) % BLOCKS).astype(jnp.int32)
            query_part, key_portion, value_part = block_grads(query_heads, gradient_per_head, lse_heads, delta_per_head,
                                                           key_blocks[source], value_blocks[source], score_scale)
            query_sum = query_sum + query_part
            key_list.append(key_portion)
            value_list.append(value_part)
        query_low = (score_scale * query_sum).astype(jnp.bfloat16)
        return query_low, jnp.stack(key_list), jnp.stack(value_list)

    query_low, key_parts, value_parts = lax.map(one_block, jnp.arange(BLOCKS, dtype=jnp.int32))
    key_total = jnp.zeros((BLOCKS, BLK, KVHEADS, HEAD_DIM), jnp.float32)
    value_total = jnp.zeros((BLOCKS, BLK, KVHEADS, HEAD_DIM), jnp.float32)
    for offset in range(STEPS):
        key_total = key_total + jnp.roll(key_parts[:, offset], -offset, axis=0)
        value_total = value_total + jnp.roll(value_parts[:, offset], -offset, axis=0)
    query_gradient = query_low.reshape(SEQ, QHEADS * HEAD_DIM)
    key_grad = (score_scale * key_total).astype(jnp.bfloat16).reshape(SEQ, KVHEADS * HEAD_DIM)
    value_grad = value_total.astype(jnp.bfloat16).reshape(SEQ, KVHEADS * HEAD_DIM)
    return query_gradient, key_grad, value_grad
```

```python
import functools

import jax
import jax.numpy as jnp
from jax import lax
from jax.experimental import pallas as pl
from jax.experimental.pallas import tpu as pltpu
from jax.sharding import PartitionSpec as P

QHEADS = 40
KVHEADS = 8
HEAD_DIM = 128
STEPS = 3
GROUP = QHEADS // KVHEADS
SCALE = HEAD_DIM ** (-0.5)

VMEM = pl.BlockSpec(memory_space=pltpu.VMEM)
ANY = pl.BlockSpec(memory_space=pl.ANY)
PARAMS = pltpu.CompilerParams(vmem_limit_bytes=16 * 1024 * 1024)


def shifted(array, axis, by):
    size = lax.axis_size(axis)
    return lax.ppermute(array, axis, [(i, (i + by) % size) for i in range(size)])


def is_power(n):
    return n & (n - 1) == 0


def partner(me, step, n, back=False):
    if is_power(n):
        return lax.bitwise_xor(me, step)
    return lax.rem(me + (n - step if back else step), n)


def exchange(array, axis, step):
    n = lax.axis_size(axis)
    if is_power(n):
        pairs = [(i, i ^ step) for i in range(n)]
    else:
        pairs = [(i, (i + step) % n) for i in range(n)]
    return lax.ppermute(array, axis, pairs)


def nt(a, b):
    return lax.dot_general(a, b, (((1,), (1,)), ((), ())), preferred_element_type=jnp.float32)


def nn(a, b):
    return lax.dot_general(a, b, (((1,), (0,)), ((), ())), preferred_element_type=jnp.float32)


def tn(a, b):
    return lax.dot_general(a, b, (((0,), (0,)), ((), ())), preferred_element_type=jnp.float32)


def prep_kernel(n, grad, key, value, *refs):
    sends, kv, sems = refs[: n - 1], refs[n - 1], refs[n]
    me = lax.axis_index("uly")
    width = sends[0].shape[1]
    tokens = key.shape[0]
    copies = []
    for step in range(1, n):
        to = partner(me, step, n)
        columns = pl.ds(pl.multiple_of(to * width, width), width)
        copies.append(
            pltpu.make_async_copy(grad.at[:, columns], sends[step - 1], sems.at[step - 1])
        )
    copies.append(pltpu.make_async_copy(key, kv.at[pl.ds(0, tokens)], sems.at[n - 1]))
    copies.append(pltpu.make_async_copy(value, kv.at[pl.ds(tokens, tokens)], sems.at[n]))
    for copy in copies:
        copy.start()
    for copy in copies:
        copy.wait()


def heads_of(ref, g):
    return jnp.concatenate(
        [
            ref[:, pl.ds((g * GROUP + h) * HEAD_DIM, HEAD_DIM)]
            for h in range(GROUP)
        ],
        axis=0,
    )


def main_kernel(n, query, output, lse, grad, key, value, *refs):
    moved = refs[: STEPS - 1]
    received = refs[STEPS - 1 : STEPS - 1 + n - 1]
    rest = refs[STEPS - 1 + n - 1 :]
    far = rest[: STEPS - 1]
    own, dscore, gathered = rest[STEPS - 1 :]
    me = lax.axis_index("uly")
    rows = grad.shape[0]
    width = query.shape[1]
    tokens = query.shape[0]
    kv_local = key.shape[1] // HEAD_DIM
    columns = pl.ds(pl.multiple_of(me * width, width), width)
    gathered[pl.ds(pl.multiple_of(me * rows, rows), rows), :] = grad[:, columns]
    for step in range(1, n):
        source = partner(me, step, n, back=True)
        gathered[pl.ds(pl.multiple_of(source * rows, rows), rows), :] = received[step - 1][...]
    ones = jnp.ones((8, HEAD_DIM), jnp.bfloat16)
    for g in range(kv_local):
        cols = pl.ds(g * HEAD_DIM, HEAD_DIM)
        q = heads_of(query, g)
        go = heads_of(gathered, g)
        o = heads_of(output, g)
        k = jnp.concatenate([key[:, cols]] + [m[pl.ds(0, tokens), cols] for m in moved], axis=0)
        v = jnp.concatenate([value[:, cols]] + [m[pl.ds(tokens, tokens), cols] for m in moved], axis=0)
        product = go.astype(jnp.float32) * o.astype(jnp.float32)
        high = product.astype(jnp.bfloat16)
        low = (product - high.astype(jnp.float32)).astype(jnp.bfloat16)
        delta = (nt(ones, high) + nt(ones, low))[0:1, :]
        lse_row = jnp.concatenate(
            [lse[pl.ds(g * GROUP + h, 1), :] for h in range(GROUP)], axis=1
        )
        prob = jnp.exp(nt(k, q) * SCALE - lse_row)
        ds = (prob * (nt(v, go) - delta)).astype(jnp.bfloat16)
        dv = nn(prob.astype(jnp.bfloat16), go)
        dk = nn(ds, q) * SCALE
        dscore[g] = ds
        own[pl.ds(0, tokens), cols] = dk[:tokens]
        own[pl.ds(tokens, tokens), cols] = dv[:tokens]
        for i in range(1, STEPS):
            part = slice(i * tokens, (i + 1) * tokens)
            far[i - 1][pl.ds(0, tokens), cols] = dk[part].astype(jnp.bfloat16)
            far[i - 1][pl.ds(tokens, tokens), cols] = dv[part].astype(jnp.bfloat16)


def query_kernel(dscore, key, *refs):
    moved, out = refs[: STEPS - 1], refs[STEPS - 1]
    tokens = key.shape[0]
    kv_local = key.shape[1] // HEAD_DIM
    for g in range(kv_local):
        cols = pl.ds(g * HEAD_DIM, HEAD_DIM)
        k = jnp.concatenate([key[:, cols]] + [m[pl.ds(0, tokens), cols] for m in moved], axis=0)
        dq = (tn(dscore[g], k) * SCALE).astype(jnp.bfloat16)
        for h in range(GROUP):
            out[:, pl.ds((g * GROUP + h) * HEAD_DIM, HEAD_DIM)] = dq[h * tokens : (h + 1) * tokens]


def sum_kernel(n, dq, own, *refs):
    back = refs[: STEPS - 1]
    sends, total = refs[STEPS - 1 : -1], refs[-1]
    me = lax.axis_index("uly")
    width = dq.shape[1]
    kv_width = own.shape[1]
    tokens = dq.shape[0]
    rows = tokens // n
    acc = own[...]
    for b in back:
        acc = acc + b[...].astype(jnp.float32)
    total[...] = acc.astype(jnp.bfloat16)
    for step in range(n):
        to = partner(me, step, n) if step else me
        start = pl.multiple_of(to * rows, rows)
        sends[step][:, pl.ds(0, width)] = dq[pl.ds(start, rows), :]
        sends[step][:, pl.ds(width, kv_width)] = total[pl.ds(start, rows), :]
        sends[step][:, pl.ds(width + kv_width, kv_width)] = total[
            pl.ds(pl.multiple_of(start + tokens, rows), rows), :
        ]


def place_kernel(n, *refs):
    parts, (dq, dk, dv, sems) = refs[:n], refs[n:]
    me = lax.axis_index("uly")
    width = dq.shape[1] // n
    kv_width = dk.shape[1] // n
    copies = []
    for step in range(n):
        source = partner(me, step, n, back=True) if step else me
        part = parts[step]
        for i, (out, first, size) in enumerate(
            ((dq, 0, width), (dk, width, kv_width), (dv, width + kv_width, kv_width))
        ):
            columns = pl.ds(pl.multiple_of(source * size, size), size)
            copies.append(
                pltpu.make_async_copy(
                    part.at[:, pl.ds(first, size)], out.at[:, columns], sems.at[step, i]
                )
            )
    for copy in copies:
        copy.start()
    for copy in copies:
        copy.wait()


def shape(dims, kind=jnp.bfloat16):
    return jax.ShapeDtypeStruct(dims, kind)


def body(query, key, value, output, grad, lse):
    n = lax.axis_size("uly")
    tokens, width = query.shape
    kv_width = key.shape[1]
    kv_local = kv_width // HEAD_DIM
    rows = grad.shape[0]
    *sends, kv = pl.pallas_call(
        functools.partial(prep_kernel, n),
        out_shape=[shape((rows, width))] * (n - 1) + [shape((2 * tokens, kv_width))],
        in_specs=[ANY] * 3,
        out_specs=[ANY] * n,
        scratch_shapes=[pltpu.SemaphoreType.DMA((n + 1,))],
        compiler_params=PARAMS,
        name="prep",
    )(grad, key, value)
    received = [exchange(sends[step - 1], "uly", step) for step in range(1, n)]
    moved = [shifted(kv, "blk", i) for i in range(1, STEPS)]
    *far, own, dscore = pl.pallas_call(
        functools.partial(main_kernel, n),
        out_shape=[shape((2 * tokens, kv_width))] * (STEPS - 1)
        + [
            shape((2 * tokens, kv_width), jnp.float32),
            shape((kv_local, STEPS * tokens, GROUP * tokens)),
        ],
        in_specs=[VMEM] * (6 + STEPS - 1 + n - 1),
        out_specs=[VMEM] * (STEPS + 1),
        scratch_shapes=[pltpu.VMEM((tokens, width), jnp.bfloat16)],
        compiler_params=PARAMS,
        name="main",
    )(query, output, lse, grad, key, value, *moved, *received)
    back = [shifted(far[i - 1], "blk", -i) for i in range(1, STEPS)]
    dq = pl.pallas_call(
        query_kernel,
        out_shape=shape((tokens, width)),
        in_specs=[VMEM] * (STEPS + 1),
        out_specs=VMEM,
        compiler_params=PARAMS,
        name="query",
    )(dscore, key, *moved)
    parts = pl.pallas_call(
        functools.partial(sum_kernel, n),
        out_shape=[shape((rows, width + 2 * kv_width))] * n,
        in_specs=[VMEM] * (STEPS + 1),
        out_specs=[VMEM] * n,
        scratch_shapes=[pltpu.VMEM((2 * tokens, kv_width), jnp.bfloat16)],
        compiler_params=PARAMS,
        name="sum",
    )(dq, own, *back)
    final = [parts[0]] + [exchange(parts[step], "uly", step) for step in range(1, n)]
    return pl.pallas_call(
        functools.partial(place_kernel, n),
        out_shape=[
            shape((rows, width * n)),
            shape((rows, kv_width * n)),
            shape((rows, kv_width * n)),
        ],
        in_specs=[ANY] * n,
        out_specs=[ANY] * 3,
        scratch_shapes=[pltpu.SemaphoreType.DMA((n, 3))],
        compiler_params=PARAMS,
        name="place",
    )(*final)


def solution(mesh):
    placed = (
        P("blk", "uly"),
        P("blk", "uly"),
        P("blk", "uly"),
        P("blk", "uly"),
        P(("blk", "uly"), None),
        P("uly", "blk"),
    )
    return jax.shard_map(
        lambda *args: tuple(body(*args)),
        mesh=mesh,
        in_specs=placed,
        out_specs=(P(("blk", "uly"), None), P(("blk", "uly"), None), P(("blk", "uly"), None)),
        check_vma=False,
    )
```

```python
import functools

import jax
import jax.numpy as jnp
from jax import lax
from jax.experimental import pallas as pl
from jax.experimental.pallas import tpu as pltpu
from jax.sharding import PartitionSpec as P

QHEADS = 40
KVHEADS = 8
HEAD_DIM = 128
STEPS = 3
GROUP = QHEADS // KVHEADS
SCALE = HEAD_DIM ** (-0.5)

VMEM = pl.BlockSpec(memory_space=pltpu.VMEM)
ANY = pl.BlockSpec(memory_space=pl.ANY)
HBM = pl.BlockSpec(memory_space=pltpu.HBM)
PARAMS = pltpu.CompilerParams(vmem_limit_bytes=16 * 1024 * 1024)


def shifted(array, axis, by):
    size = lax.axis_size(axis)
    return lax.ppermute(array, axis, [(i, (i + by) % size) for i in range(size)])


def is_power(n):
    return n & (n - 1) == 0


def partner(me, step, n, back=False):
    if is_power(n):
        return lax.bitwise_xor(me, step)
    return lax.rem(me + (n - step if back else step), n)


def exchange(array, axis, step):
    n = lax.axis_size(axis)
    if is_power(n):
        pairs = [(i, i ^ step) for i in range(n)]
    else:
        pairs = [(i, (i + step) % n) for i in range(n)]
    return lax.ppermute(array, axis, pairs)


def nt(a, b):
    return lax.dot_general(a, b, (((1,), (1,)), ((), ())), preferred_element_type=jnp.float32)


def nn(a, b):
    return lax.dot_general(a, b, (((1,), (0,)), ((), ())), preferred_element_type=jnp.float32)


def tn(a, b):
    return lax.dot_general(a, b, (((0,), (0,)), ((), ())), preferred_element_type=jnp.float32)


def prep_kernel(n, grad, key, value, *refs):
    slices, kv, sems = refs[:n], refs[n], refs[n + 1]
    me = lax.axis_index("uly")
    width = slices[0].shape[1]
    tokens = key.shape[0]
    copies = [
        pltpu.make_async_copy(key, kv.at[pl.ds(0, tokens)], sems.at[n]),
        pltpu.make_async_copy(value, kv.at[pl.ds(tokens, tokens)], sems.at[n + 1]),
    ]
    for step in range(n):
        to = partner(me, step, n) if step else me
        columns = pl.ds(pl.multiple_of(to * width, width), width)
        copies.append(pltpu.make_async_copy(grad.at[:, columns], slices[step], sems.at[step]))
    for copy in copies:
        copy.start()
    for copy in copies:
        copy.wait()


def early_kernel(query, output, lse, key, value, *refs):
    moved, refs = refs[: STEPS - 1], refs[STEPS - 1 :]
    prob, queries, outputs, keys, values, query_in, output_in, lse_in, sems = refs
    tokens = key.shape[0]
    kv_local = key.shape[1] // HEAD_DIM
    copies = [
        pltpu.make_async_copy(query, query_in, sems.at[0]),
        pltpu.make_async_copy(output, output_in, sems.at[1]),
        pltpu.make_async_copy(lse, lse_in, sems.at[2]),
    ]
    for g in range(kv_local):
        cols = pl.ds(g * HEAD_DIM, HEAD_DIM)
        own = pl.ds(0, tokens)
        copies.append(pltpu.make_async_copy(key.at[:, cols], keys.at[g, own], sems.at[3 + 2 * g]))
        copies.append(pltpu.make_async_copy(value.at[:, cols], values.at[g, own], sems.at[4 + 2 * g]))
    for copy in copies:
        copy.start()
    for g in range(kv_local):
        cols = pl.ds(g * HEAD_DIM, HEAD_DIM)
        for i in range(1, STEPS):
            part = pl.ds(i * tokens, tokens)
            keys[g, part] = moved[i - 1][pl.ds(0, tokens), cols]
            values[g, part] = moved[i - 1][pl.ds(tokens, tokens), cols]
    for copy in copies:
        copy.wait()
    for g in range(kv_local):
        for h in range(GROUP):
            head = pl.ds((g * GROUP + h) * HEAD_DIM, HEAD_DIM)
            part = pl.ds(h * tokens, tokens)
            queries[g, part] = query_in[:, head]
            outputs[g, part] = output_in[:, head]
        lse_row = jnp.concatenate(
            [lse_in[pl.ds(g * GROUP + h, 1), :] for h in range(GROUP)], axis=1
        )
        prob[g] = jnp.exp(nt(keys[g], queries[g]) * SCALE - lse_row)


def main_kernel(n, prob, queries, outputs, keys, values, mine, *refs):
    received = refs[: n - 1][::-1]
    rest = refs[n - 1 :]
    far = rest[: STEPS - 1]
    own, dscore, stacked = rest[STEPS - 1 :]
    me = lax.axis_index("uly")
    rows = mine.shape[0]
    tokens = rows * n
    kv_local = prob.shape[0]
    for step in range(n):
        source = partner(me, step, n, back=True) if step else me
        piece = received[step - 1] if step else mine
        start = pl.multiple_of(source * rows, rows)
        for g in range(kv_local):
            for h in range(GROUP):
                stacked[g, pl.ds(start + h * tokens, rows)] = piece[
                    :, pl.ds((g * GROUP + h) * HEAD_DIM, HEAD_DIM)
                ]
    ones = jnp.ones((8, HEAD_DIM), jnp.bfloat16)
    for g in range(kv_local):
        cols = pl.ds(g * HEAD_DIM, HEAD_DIM)
        go = stacked[g]
        product = go.astype(jnp.float32) * outputs[g].astype(jnp.float32)
        high = product.astype(jnp.bfloat16)
        low = (product - high.astype(jnp.float32)).astype(jnp.bfloat16)
        delta = (nt(ones, high) + nt(ones, low))[0:1, :]
        p = prob[g]
        ds = (p * (nt(values[g], go) - delta)).astype(jnp.bfloat16)
        dv = nn(p.astype(jnp.bfloat16), go)
        dk = nn(ds, queries[g]) * SCALE
        dscore[g] = ds
        own[pl.ds(0, tokens), cols] = dk[:tokens]
        own[pl.ds(tokens, tokens), cols] = dv[:tokens]
        for i in range(1, STEPS):
            part = slice(i * tokens, (i + 1) * tokens)
            far[i - 1][pl.ds(0, tokens), cols] = dk[part].astype(jnp.bfloat16)
            far[i - 1][pl.ds(tokens, tokens), cols] = dv[part].astype(jnp.bfloat16)


def query_kernel(dscore, keys, out):
    tokens = out.shape[0]
    for g in range(dscore.shape[0]):
        dq = (tn(dscore[g], keys[g]) * SCALE).astype(jnp.bfloat16)
        for h in range(GROUP):
            out[:, pl.ds((g * GROUP + h) * HEAD_DIM, HEAD_DIM)] = dq[h * tokens : (h + 1) * tokens]


def sum_kernel(n, dq, own, *refs):
    back = refs[: STEPS - 1]
    sends, total = refs[STEPS - 1 : -1], refs[-1]
    me = lax.axis_index("uly")
    width = dq.shape[1]
    kv_width = own.shape[1]
    tokens = dq.shape[0]
    rows = tokens // n
    acc = own[...]
    for b in back:
        acc = acc + b[...].astype(jnp.float32)
    total[...] = acc.astype(jnp.bfloat16)
    for step in range(n):
        to = partner(me, step, n) if step else me
        start = pl.multiple_of(to * rows, rows)
        sends[step][:, pl.ds(0, width)] = dq[pl.ds(start, rows), :]
        sends[step][:, pl.ds(width, kv_width)] = total[pl.ds(start, rows), :]
        sends[step][:, pl.ds(width + kv_width, kv_width)] = total[
            pl.ds(pl.multiple_of(start + tokens, rows), rows), :
        ]


def place_kernel(n, *refs):
    parts, (dq, dk, dv, sems) = refs[:n][::-1], refs[n:]
    me = lax.axis_index("uly")
    width = dq.shape[1] // n
    kv_width = dk.shape[1] // n
    copies = []
    for step in range(n):
        source = partner(me, step, n, back=True) if step else me
        part = parts[step]
        for i, (out, first, size) in enumerate(
            ((dq, 0, width), (dk, width, kv_width), (dv, width + kv_width, kv_width))
        ):
            columns = pl.ds(pl.multiple_of(source * size, size), size)
            copies.append(
                pltpu.make_async_copy(
                    part.at[:, pl.ds(first, size)], out.at[:, columns], sems.at[step, i]
                )
            )
    for copy in copies:
        copy.start()
    for copy in copies:
        copy.wait()


def shape(dims, kind=jnp.bfloat16):
    return jax.ShapeDtypeStruct(dims, kind)


def body(query, key, value, output, grad, lse):
    n = lax.axis_size("uly")
    tokens, width = query.shape
    kv_width = key.shape[1]
    kv_local = kv_width // HEAD_DIM
    rows = grad.shape[0]
    key_rows, query_rows = STEPS * tokens, GROUP * tokens
    query, output, lse, grad, key, value = (
        pltpu.with_memory_space_constraint(a, pltpu.HBM)
        for a in (query, output, lse, grad, key, value)
    )
    *slices, kv = pl.pallas_call(
        functools.partial(prep_kernel, n),
        out_shape=[shape((rows, width))] * n + [shape((2 * tokens, kv_width))],
        in_specs=[HBM] * 3,
        out_specs=[ANY] * (n + 1),
        scratch_shapes=[pltpu.SemaphoreType.DMA((n + 2,))],
        compiler_params=PARAMS,
        name="prep",
    )(grad, key, value)
    received = [exchange(slices[step], "uly", step) for step in range(1, n)]
    moved = [shifted(kv, "blk", i) for i in range(1, STEPS)]
    early = pl.pallas_call(
        early_kernel,
        out_shape=[
            shape((kv_local, key_rows, query_rows), jnp.float32),
            shape((kv_local, query_rows, HEAD_DIM)),
            shape((kv_local, query_rows, HEAD_DIM)),
            shape((kv_local, key_rows, HEAD_DIM)),
            shape((kv_local, key_rows, HEAD_DIM)),
        ],
        in_specs=[HBM] * 5 + [VMEM] * (STEPS - 1),
        out_specs=[VMEM] * 5,
        scratch_shapes=[
            pltpu.VMEM((tokens, width), jnp.bfloat16),
            pltpu.VMEM((tokens, width), jnp.bfloat16),
            pltpu.VMEM(lse.shape, jnp.float32),
            pltpu.SemaphoreType.DMA((3 + 2 * kv_local,)),
        ],
        compiler_params=PARAMS,
        name="early",
    )(query, output, lse, key, value, *moved)
    *far, own, dscore = pl.pallas_call(
        functools.partial(main_kernel, n),
        out_shape=[shape((2 * tokens, kv_width))] * (STEPS - 1)
        + [shape((2 * tokens, kv_width), jnp.float32), shape((kv_local, key_rows, query_rows))],
        in_specs=[VMEM] * (6 + n - 1),
        out_specs=[VMEM] * (STEPS + 1),
        scratch_shapes=[pltpu.VMEM((kv_local, query_rows, HEAD_DIM), jnp.bfloat16)],
        compiler_params=PARAMS,
        name="main",
    )(*early, slices[0], *received[::-1])
    back = [shifted(far[i - 1], "blk", -i) for i in range(STEPS - 1, 0, -1)]
    dq = pl.pallas_call(
        query_kernel,
        out_shape=shape((tokens, width)),
        in_specs=[VMEM] * 2,
        out_specs=VMEM,
        compiler_params=PARAMS,
        name="query",
    )(dscore, early[3])
    parts = pl.pallas_call(
        functools.partial(sum_kernel, n),
        out_shape=[shape((rows, width + 2 * kv_width))] * n,
        in_specs=[VMEM] * (STEPS + 1),
        out_specs=[VMEM] * n,
        scratch_shapes=[pltpu.VMEM((2 * tokens, kv_width), jnp.bfloat16)],
        compiler_params=PARAMS,
        name="sum",
    )(dq, own, *back)
    final = [parts[0]] + [exchange(parts[step], "uly", step) for step in range(1, n)]
    return pl.pallas_call(
        functools.partial(place_kernel, n),
        out_shape=[
            shape((rows, width * n)),
            shape((rows, kv_width * n)),
            shape((rows, kv_width * n)),
        ],
        in_specs=[ANY] * n,
        out_specs=[HBM] * 3,
        scratch_shapes=[pltpu.SemaphoreType.DMA((n, 3))],
        compiler_params=PARAMS,
        name="place",
    )(*final[::-1])


def solution(mesh):
    placed = (
        P("blk", "uly"),
        P("blk", "uly"),
        P("blk", "uly"),
        P("blk", "uly"),
        P(("blk", "uly"), None),
        P("uly", "blk"),
    )
    return jax.shard_map(
        lambda *args: tuple(body(*args)),
        mesh=mesh,
        in_specs=placed,
        out_specs=(P(("blk", "uly"), None), P(("blk", "uly"), None), P(("blk", "uly"), None)),
        check_vma=False,
    )
```

```python
import functools

import jax
import jax.numpy as jnp
from jax import lax
from jax.experimental import pallas as pl
from jax.experimental.pallas import tpu as pltpu
from jax.sharding import PartitionSpec as P

QHEADS = 40
KVHEADS = 8
HEAD_DIM = 128
STEPS = 3
GROUP = QHEADS // KVHEADS
SCALE = HEAD_DIM ** (-0.5)
AHEAD = (2,)

VMEM = pl.BlockSpec(memory_space=pltpu.VMEM)
ANY = pl.BlockSpec(memory_space=pl.ANY)
HBM = pl.BlockSpec(memory_space=pltpu.HBM)
PARAMS = pltpu.CompilerParams(vmem_limit_bytes=16 * 1024 * 1024)


def shifted(array, axis, by):
    size = lax.axis_size(axis)
    return lax.ppermute(array, axis, [(i, (i + by) % size) for i in range(size)])


def is_power(n):
    return n & (n - 1) == 0


def partner(me, step, n, back=False):
    if is_power(n):
        return lax.bitwise_xor(me, step)
    return lax.rem(me + (n - step if back else step), n)


def exchange(array, axis, step):
    n = lax.axis_size(axis)
    if is_power(n):
        pairs = [(i, i ^ step) for i in range(n)]
    else:
        pairs = [(i, (i + step) % n) for i in range(n)]
    return lax.ppermute(array, axis, pairs)


def nt(a, b):
    return lax.dot_general(a, b, (((1,), (1,)), ((), ())), preferred_element_type=jnp.float32)


def nn(a, b):
    return lax.dot_general(a, b, (((1,), (0,)), ((), ())), preferred_element_type=jnp.float32)


def tn(a, b):
    return lax.dot_general(a, b, (((0,), (0,)), ((), ())), preferred_element_type=jnp.float32)


def prep_kernel(n, grad, key, value, *refs):
    slices, kv, sems = refs[:n], refs[n], refs[n + 1]
    me = lax.axis_index("uly")
    width = slices[0].shape[1]
    tokens = key.shape[0]
    copies = [
        pltpu.make_async_copy(key, kv.at[pl.ds(0, tokens)], sems.at[n]),
        pltpu.make_async_copy(value, kv.at[pl.ds(tokens, tokens)], sems.at[n + 1]),
    ]
    for step in range(n):
        to = partner(me, step, n) if step else me
        columns = pl.ds(pl.multiple_of(to * width, width), width)
        copies.append(pltpu.make_async_copy(grad.at[:, columns], slices[step], sems.at[step]))
    for copy in copies:
        copy.start()
    for copy in copies:
        copy.wait()


def early_kernel(query, output, lse, key, value, *refs):
    moved, refs = refs[: STEPS - 1], refs[STEPS - 1 :]
    prob, queries, outputs, keys, values, query_in, output_in, lse_in, sems = refs
    tokens = key.shape[0]
    kv_local = key.shape[1] // HEAD_DIM
    copies = [
        pltpu.make_async_copy(query, query_in, sems.at[0]),
        pltpu.make_async_copy(output, output_in, sems.at[1]),
        pltpu.make_async_copy(lse, lse_in, sems.at[2]),
    ]
    for g in range(kv_local):
        cols = pl.ds(g * HEAD_DIM, HEAD_DIM)
        own = pl.ds(0, tokens)
        copies.append(pltpu.make_async_copy(key.at[:, cols], keys.at[g, own], sems.at[3 + 2 * g]))
        copies.append(pltpu.make_async_copy(value.at[:, cols], values.at[g, own], sems.at[4 + 2 * g]))
    for copy in copies:
        copy.start()
    for g in range(kv_local):
        cols = pl.ds(g * HEAD_DIM, HEAD_DIM)
        for i in range(1, STEPS):
            part = pl.ds(i * tokens, tokens)
            keys[g, part] = moved[i - 1][pl.ds(0, tokens), cols]
            values[g, part] = moved[i - 1][pl.ds(tokens, tokens), cols]
    for copy in copies:
        copy.wait()
    for g in range(kv_local):
        for h in range(GROUP):
            head = pl.ds((g * GROUP + h) * HEAD_DIM, HEAD_DIM)
            part = pl.ds(h * tokens, tokens)
            queries[g, part] = query_in[:, head]
            outputs[g, part] = output_in[:, head]
        lse_row = jnp.concatenate(
            [lse_in[pl.ds(g * GROUP + h, 1), :] for h in range(GROUP)], axis=1
        )
        prob[g] = jnp.exp(nt(keys[g], queries[g]) * SCALE - lse_row)


def main_kernel(n, prob, queries, outputs, keys, values, mine, *refs):
    received = refs[: n - 1][::-1]
    rest = refs[n - 1 :]
    far = rest[: STEPS - 1]
    own, dscore, stacked = rest[STEPS - 1 :]
    me = lax.axis_index("uly")
    rows = mine.shape[0]
    tokens = rows * n
    kv_local = prob.shape[0]
    for step in range(n):
        source = partner(me, step, n, back=True) if step else me
        piece = received[step - 1] if step else mine
        start = pl.multiple_of(source * rows, rows)
        for g in range(kv_local):
            for h in range(GROUP):
                stacked[g, pl.ds(start + h * tokens, rows)] = piece[
                    :, pl.ds((g * GROUP + h) * HEAD_DIM, HEAD_DIM)
                ]
    ones = jnp.ones((8, HEAD_DIM), jnp.bfloat16)
    for g in range(kv_local):
        cols = pl.ds(g * HEAD_DIM, HEAD_DIM)
        go = stacked[g]
        product = go.astype(jnp.float32) * outputs[g].astype(jnp.float32)
        high = product.astype(jnp.bfloat16)
        low = (product - high.astype(jnp.float32)).astype(jnp.bfloat16)
        delta = (nt(ones, high) + nt(ones, low))[0:1, :]
        p = prob[g]
        ds = (p * (nt(values[g], go) - delta)).astype(jnp.bfloat16)
        dv = nn(p.astype(jnp.bfloat16), go)
        dk = nn(ds, queries[g]) * SCALE
        dscore[g] = ds
        own[pl.ds(0, tokens), cols] = dk[:tokens]
        own[pl.ds(tokens, tokens), cols] = dv[:tokens]
        for i in range(1, STEPS):
            part = slice(i * tokens, (i + 1) * tokens)
            far[i - 1][pl.ds(0, tokens), cols] = dk[part].astype(jnp.bfloat16)
            far[i - 1][pl.ds(tokens, tokens), cols] = dv[part].astype(jnp.bfloat16)


def query_kernel(n, dscore, keys, out, *sends):
    tokens = out.shape[0]
    rows = tokens // n
    for g in range(dscore.shape[0]):
        dq = (tn(dscore[g], keys[g]) * SCALE).astype(jnp.bfloat16)
        for h in range(GROUP):
            out[:, pl.ds((g * GROUP + h) * HEAD_DIM, HEAD_DIM)] = dq[h * tokens : (h + 1) * tokens]
    me = lax.axis_index("uly")
    for step, send in zip(AHEAD, sends):
        start = pl.multiple_of(partner(me, step, n) * rows, rows)
        send[...] = out[pl.ds(start, rows), :]


def sum_kernel(n, dq, own, *refs):
    back = refs[: STEPS - 1]
    sends, total = refs[STEPS - 1 : -1], refs[-1]
    me = lax.axis_index("uly")
    width = dq.shape[1]
    kv_width = own.shape[1]
    tokens = dq.shape[0]
    rows = tokens // n
    acc = own[...]
    for b in back:
        acc = acc + b[...].astype(jnp.float32)
    total[...] = acc.astype(jnp.bfloat16)
    for step in range(n):
        to = partner(me, step, n) if step else me
        start = pl.multiple_of(to * rows, rows)
        first = 0 if step in AHEAD else width
        if first:
            sends[step][:, pl.ds(0, width)] = dq[pl.ds(start, rows), :]
        sends[step][:, pl.ds(first, kv_width)] = total[pl.ds(start, rows), :]
        sends[step][:, pl.ds(first + kv_width, kv_width)] = total[
            pl.ds(pl.multiple_of(start + tokens, rows), rows), :
        ]


def pack_kernel(part, *refs):
    refs[-1][...] = part[...]


def place_kernel(n, *refs):
    parts, refs = refs[:n][::-1], refs[n:]
    ahead, (dq, dk, dv, sems) = refs[: len(AHEAD)], refs[len(AHEAD) :]
    me = lax.axis_index("uly")
    width = dq.shape[1] // n
    kv_width = dk.shape[1] // n
    copies = []
    for step in range(n):
        source = partner(me, step, n, back=True) if step else me
        first = 0 if step in AHEAD else width
        pieces = (
            (dk, parts[step], first, kv_width),
            (dv, parts[step], first + kv_width, kv_width),
            (dq, ahead[AHEAD.index(step)] if step in AHEAD else parts[step], 0, width),
        )
        for i, (out, part, at, size) in enumerate(pieces):
            columns = pl.ds(pl.multiple_of(source * size, size), size)
            copies.append(
                pltpu.make_async_copy(
                    part.at[:, pl.ds(at, size)], out.at[:, columns], sems.at[step, i]
                )
            )
    for copy in copies:
        copy.start()
    for copy in copies:
        copy.wait()


def shape(dims, kind=jnp.bfloat16):
    return jax.ShapeDtypeStruct(dims, kind)


def body(query, key, value, output, grad, lse):
    n = lax.axis_size("uly")
    tokens, width = query.shape
    kv_width = key.shape[1]
    kv_local = kv_width // HEAD_DIM
    rows = grad.shape[0]
    key_rows, query_rows = STEPS * tokens, GROUP * tokens
    query, output, lse, grad, key, value = (
        pltpu.with_memory_space_constraint(a, pltpu.HBM)
        for a in (query, output, lse, grad, key, value)
    )
    *slices, kv = pl.pallas_call(
        functools.partial(prep_kernel, n),
        out_shape=[shape((rows, width))] * n + [shape((2 * tokens, kv_width))],
        in_specs=[HBM] * 3,
        out_specs=[ANY] * (n + 1),
        scratch_shapes=[pltpu.SemaphoreType.DMA((n + 2,))],
        compiler_params=PARAMS,
        name="prep",
    )(grad, key, value)
    received = [exchange(slices[step], "uly", step) for step in range(1, n)]
    moved = [shifted(kv, "blk", i) for i in range(1, STEPS)]
    early = pl.pallas_call(
        early_kernel,
        out_shape=[
            shape((kv_local, key_rows, query_rows), jnp.float32),
            shape((kv_local, query_rows, HEAD_DIM)),
            shape((kv_local, query_rows, HEAD_DIM)),
            shape((kv_local, key_rows, HEAD_DIM)),
            shape((kv_local, key_rows, HEAD_DIM)),
        ],
        in_specs=[HBM] * 5 + [VMEM] * (STEPS - 1),
        out_specs=[VMEM] * 5,
        scratch_shapes=[
            pltpu.VMEM((tokens, width), jnp.bfloat16),
            pltpu.VMEM((tokens, width), jnp.bfloat16),
            pltpu.VMEM(lse.shape, jnp.float32),
            pltpu.SemaphoreType.DMA((3 + 2 * kv_local,)),
        ],
        compiler_params=PARAMS,
        name="early",
    )(query, output, lse, key, value, *moved)
    *far, own, dscore = pl.pallas_call(
        functools.partial(main_kernel, n),
        out_shape=[shape((2 * tokens, kv_width))] * (STEPS - 1)
        + [shape((2 * tokens, kv_width), jnp.float32), shape((kv_local, key_rows, query_rows))],
        in_specs=[VMEM] * (6 + n - 1),
        out_specs=[VMEM] * (STEPS + 1),
        scratch_shapes=[pltpu.VMEM((kv_local, query_rows, HEAD_DIM), jnp.bfloat16)],
        compiler_params=PARAMS,
        name="main",
    )(*early, slices[0], *received[::-1])
    back = [shifted(far[i - 1], "blk", -i) for i in range(STEPS - 1, 0, -1)]
    dq, *ahead = pl.pallas_call(
        functools.partial(query_kernel, n),
        out_shape=[shape((tokens, width))] + [shape((rows, width))] * len(AHEAD),
        in_specs=[VMEM] * 2,
        out_specs=[VMEM] * (1 + len(AHEAD)),
        compiler_params=PARAMS,
        name="query",
    )(dscore, early[3])
    ahead = [exchange(a, "uly", step) for a, step in zip(ahead, AHEAD)]
    *parts, = pl.pallas_call(
        functools.partial(sum_kernel, n),
        out_shape=[
            shape((rows, 2 * kv_width + (0 if step in AHEAD else width))) for step in range(n)
        ],
        in_specs=[VMEM] * (STEPS + 1),
        out_specs=[VMEM] * n,
        scratch_shapes=[pltpu.VMEM((2 * tokens, kv_width), jnp.bfloat16)],
        compiler_params=PARAMS,
        name="sum",
    )(dq, own, *back)
    if AHEAD:
        parts[AHEAD[-1]] = pl.pallas_call(
            pack_kernel,
            out_shape=shape(parts[AHEAD[-1]].shape),
            in_specs=[VMEM] + [ANY] * len(AHEAD),
            out_specs=VMEM,
            compiler_params=PARAMS,
            name="pack",
        )(parts[AHEAD[-1]], *ahead)
    final = [parts[0]] + [exchange(parts[step], "uly", step) for step in range(1, n)]
    return pl.pallas_call(
        functools.partial(place_kernel, n),
        out_shape=[
            shape((rows, width * n)),
            shape((rows, kv_width * n)),
            shape((rows, kv_width * n)),
        ],
        in_specs=[ANY] * (n + len(AHEAD)),
        out_specs=[HBM] * 3,
        scratch_shapes=[pltpu.SemaphoreType.DMA((n, 3))],
        compiler_params=PARAMS,
        name="place",
    )(*final[::-1], *ahead)


def solution(mesh):
    placed = (
        P("blk", "uly"),
        P("blk", "uly"),
        P("blk", "uly"),
        P("blk", "uly"),
        P(("blk", "uly"), None),
        P("uly", "blk"),
    )
    return jax.shard_map(
        lambda *args: tuple(body(*args)),
        mesh=mesh,
        in_specs=placed,
        out_specs=(P(("blk", "uly"), None), P(("blk", "uly"), None), P(("blk", "uly"), None)),
        check_vma=False,
    )
```

```python
import functools

import jax
import jax.numpy as jnp
from jax import lax
from jax.experimental import pallas as pl
from jax.experimental.pallas import tpu as pltpu
from jax.sharding import PartitionSpec as P

QHEADS = 40
KVHEADS = 8
HEAD_DIM = 128
STEPS = 3
GROUP = QHEADS // KVHEADS
SCALE = HEAD_DIM ** (-0.5)
AHEAD = (2,)

VMEM = pl.BlockSpec(memory_space=pltpu.VMEM)
ANY = pl.BlockSpec(memory_space=pl.ANY)
HBM = pl.BlockSpec(memory_space=pltpu.HBM)
PARAMS = pltpu.CompilerParams(vmem_limit_bytes=16 * 1024 * 1024)


def shifted(array, axis, by):
    size = lax.axis_size(axis)
    return lax.ppermute(array, axis, [(i, (i + by) % size) for i in range(size)])


def is_power(n):
    return n & (n - 1) == 0


def partner(me, step, n, back=False):
    if is_power(n):
        return lax.bitwise_xor(me, step)
    return lax.rem(me + (n - step if back else step), n)


def exchange(array, axis, step):
    n = lax.axis_size(axis)
    if is_power(n):
        pairs = [(i, i ^ step) for i in range(n)]
    else:
        pairs = [(i, (i + step) % n) for i in range(n)]
    return lax.ppermute(array, axis, pairs)


def nt(a, b):
    return lax.dot_general(a, b, (((1,), (1,)), ((), ())), preferred_element_type=jnp.float32)


def nn(a, b):
    return lax.dot_general(a, b, (((1,), (0,)), ((), ())), preferred_element_type=jnp.float32)


def tn(a, b):
    return lax.dot_general(a, b, (((0,), (0,)), ((), ())), preferred_element_type=jnp.float32)


def prep_kernel(n, grad, key, value, *refs):
    slices, kv, sems = refs[:n], refs[n], refs[n + 1]
    me = lax.axis_index("uly")
    width = slices[0].shape[1]
    tokens = key.shape[0]
    copies = [
        pltpu.make_async_copy(key, kv.at[pl.ds(0, tokens)], sems.at[n]),
        pltpu.make_async_copy(value, kv.at[pl.ds(tokens, tokens)], sems.at[n + 1]),
    ]
    for step in range(n):
        to = partner(me, step, n) if step else me
        columns = pl.ds(pl.multiple_of(to * width, width), width)
        copies.append(pltpu.make_async_copy(grad.at[:, columns], slices[step], sems.at[step]))
    for copy in copies:
        copy.start()
    for copy in copies:
        copy.wait()


def early_kernel(query, output, lse, key, value, even_key, first_odd, *refs):
    moved, refs = refs[: STEPS - 2], refs[STEPS - 2 :]
    odd = lax.rem(lax.axis_index("blk"), 2) == 1
    prob, queries, outputs, keys, values, query_in, output_in, lse_in, sems = refs
    tokens = key.shape[0]
    kv_local = key.shape[1] // HEAD_DIM
    copies = [
        pltpu.make_async_copy(query, query_in, sems.at[0]),
        pltpu.make_async_copy(output, output_in, sems.at[1]),
        pltpu.make_async_copy(lse, lse_in, sems.at[2]),
    ]
    for g in range(kv_local):
        cols = pl.ds(g * HEAD_DIM, HEAD_DIM)
        own = pl.ds(0, tokens)
        copies.append(pltpu.make_async_copy(key.at[:, cols], keys.at[g, own], sems.at[3 + 2 * g]))
        copies.append(pltpu.make_async_copy(value.at[:, cols], values.at[g, own], sems.at[4 + 2 * g]))
    for copy in copies:
        copy.start()
    for g in range(kv_local):
        cols = pl.ds(g * HEAD_DIM, HEAD_DIM)
        part = pl.ds(tokens, tokens)

        @pl.when(odd)
        def _():
            keys[g, part] = first_odd[pl.ds(0, tokens), cols]
            values[g, part] = first_odd[pl.ds(tokens, tokens), cols]

        @pl.when(jnp.logical_not(odd))
        def _():
            keys[g, part] = even_key[:, cols]

        for i in range(2, STEPS):
            part = pl.ds(i * tokens, tokens)
            keys[g, part] = moved[i - 2][pl.ds(0, tokens), cols]
            values[g, part] = moved[i - 2][pl.ds(tokens, tokens), cols]
    for copy in copies:
        copy.wait()
    for g in range(kv_local):
        for h in range(GROUP):
            head = pl.ds((g * GROUP + h) * HEAD_DIM, HEAD_DIM)
            part = pl.ds(h * tokens, tokens)
            queries[g, part] = query_in[:, head]
            outputs[g, part] = output_in[:, head]
        lse_row = jnp.concatenate(
            [lse_in[pl.ds(g * GROUP + h, 1), :] for h in range(GROUP)], axis=1
        )
        prob[g] = jnp.exp(nt(keys[g], queries[g]) * SCALE - lse_row)


def halves_kernel(pair, first, second):
    rows = first.shape[0]
    first[...] = pair[pl.ds(0, rows), :]
    second[...] = pair[pl.ds(rows, rows), :]


def main_kernel(n, prob, queries, outputs, keys, values, mine, even_value, *refs):
    received = refs[: n - 1][::-1]
    rest = refs[n - 1 :]
    far = rest[: STEPS - 1]
    own, dscore, stacked = rest[STEPS - 1 :]
    me = lax.axis_index("uly")
    rows = mine.shape[0]
    tokens = rows * n
    kv_local = prob.shape[0]
    for step in range(n):
        source = partner(me, step, n, back=True) if step else me
        piece = received[step - 1] if step else mine
        start = pl.multiple_of(source * rows, rows)
        for g in range(kv_local):
            for h in range(GROUP):
                stacked[g, pl.ds(start + h * tokens, rows)] = piece[
                    :, pl.ds((g * GROUP + h) * HEAD_DIM, HEAD_DIM)
                ]
    ones = jnp.ones((8, HEAD_DIM), jnp.bfloat16)
    odd = lax.rem(lax.axis_index("blk"), 2) == 1
    for g in range(kv_local):
        cols = pl.ds(g * HEAD_DIM, HEAD_DIM)

        near = pl.ds(tokens, tokens)
        v = jnp.concatenate(
            [
                values[g, pl.ds(0, tokens)],
                jnp.where(odd, values[g, near], even_value[:, cols]),
                values[g, pl.ds(2 * tokens, (STEPS - 2) * tokens)],
            ],
            axis=0,
        )
        go = stacked[g]
        product = go.astype(jnp.float32) * outputs[g].astype(jnp.float32)
        high = product.astype(jnp.bfloat16)
        low = (product - high.astype(jnp.float32)).astype(jnp.bfloat16)
        delta = (nt(ones, high) + nt(ones, low))[0:1, :]
        p = prob[g]
        ds = (p * (nt(v, go) - delta)).astype(jnp.bfloat16)
        dv = nn(p.astype(jnp.bfloat16), go)
        dk = nn(ds, queries[g]) * SCALE
        dscore[g] = ds
        own[pl.ds(0, tokens), cols] = dk[:tokens]
        own[pl.ds(tokens, tokens), cols] = dv[:tokens]
        for i in range(1, STEPS):
            part = slice(i * tokens, (i + 1) * tokens)
            far[i - 1][pl.ds(0, tokens), cols] = dk[part].astype(jnp.bfloat16)
            far[i - 1][pl.ds(tokens, tokens), cols] = dv[part].astype(jnp.bfloat16)


def query_kernel(n, dscore, keys, out, *sends):
    tokens = out.shape[0]
    rows = tokens // n
    for g in range(dscore.shape[0]):
        dq = (tn(dscore[g], keys[g]) * SCALE).astype(jnp.bfloat16)
        for h in range(GROUP):
            out[:, pl.ds((g * GROUP + h) * HEAD_DIM, HEAD_DIM)] = dq[h * tokens : (h + 1) * tokens]
    me = lax.axis_index("uly")
    for step, send in zip(AHEAD, sends):
        start = pl.multiple_of(partner(me, step, n) * rows, rows)
        send[...] = out[pl.ds(start, rows), :]


def sum_kernel(n, dq, own, *refs):
    back = refs[: STEPS - 1]
    sends, total = refs[STEPS - 1 : -1], refs[-1]
    me = lax.axis_index("uly")
    width = dq.shape[1]
    kv_width = own.shape[1]
    tokens = dq.shape[0]
    rows = tokens // n
    acc = own[...]
    for b in back:
        acc = acc + b[...].astype(jnp.float32)
    total[...] = acc.astype(jnp.bfloat16)
    for step in range(n):
        to = partner(me, step, n) if step else me
        start = pl.multiple_of(to * rows, rows)
        first = 0 if step in AHEAD else width
        if first:
            sends[step][:, pl.ds(0, width)] = dq[pl.ds(start, rows), :]
        sends[step][:, pl.ds(first, kv_width)] = total[pl.ds(start, rows), :]
        sends[step][:, pl.ds(first + kv_width, kv_width)] = total[
            pl.ds(pl.multiple_of(start + tokens, rows), rows), :
        ]


def pack_kernel(part, *refs):
    refs[-1][...] = part[...]


def place_kernel(n, *refs):
    parts, refs = refs[:n][::-1], refs[n:]
    ahead, (dq, dk, dv, sems) = refs[: len(AHEAD)], refs[len(AHEAD) :]
    me = lax.axis_index("uly")
    width = dq.shape[1] // n
    kv_width = dk.shape[1] // n
    copies = []
    for step in range(n):
        source = partner(me, step, n, back=True) if step else me
        first = 0 if step in AHEAD else width
        pieces = (
            (dk, parts[step], first, kv_width),
            (dv, parts[step], first + kv_width, kv_width),
            (dq, ahead[AHEAD.index(step)] if step in AHEAD else parts[step], 0, width),
        )
        for i, (out, part, at, size) in enumerate(pieces):
            columns = pl.ds(pl.multiple_of(source * size, size), size)
            copies.append(
                pltpu.make_async_copy(
                    part.at[:, pl.ds(at, size)], out.at[:, columns], sems.at[step, i]
                )
            )
    for copy in copies:
        copy.start()
    for copy in copies:
        copy.wait()


def shape(dims, kind=jnp.bfloat16):
    return jax.ShapeDtypeStruct(dims, kind)


def body(query, key, value, output, grad, lse):
    n = lax.axis_size("uly")
    tokens, width = query.shape
    kv_width = key.shape[1]
    kv_local = kv_width // HEAD_DIM
    rows = grad.shape[0]
    key_rows, query_rows = STEPS * tokens, GROUP * tokens
    query, output, lse, grad, key, value = (
        pltpu.with_memory_space_constraint(a, pltpu.HBM)
        for a in (query, output, lse, grad, key, value)
    )
    *slices, kv = pl.pallas_call(
        functools.partial(prep_kernel, n),
        out_shape=[shape((rows, width))] * n + [shape((2 * tokens, kv_width))],
        in_specs=[HBM] * 3,
        out_specs=[ANY] * (n + 1),
        scratch_shapes=[pltpu.SemaphoreType.DMA((n + 2,))],
        compiler_params=PARAMS,
        name="prep",
    )(grad, key, value)
    received = [exchange(slices[step], "uly", step) for step in range(1, n)]
    moved = [shifted(kv, "blk", i) for i in range(2, STEPS)]
    swap = [(i, i ^ 1) for i in range(lax.axis_size("blk"))]
    first_odd = lax.ppermute(kv, "blk", swap)
    passed = pl.pallas_call(
        halves_kernel,
        out_shape=[shape((tokens, kv_width))] * 2,
        in_specs=[VMEM],
        out_specs=[VMEM] * 2,
        compiler_params=PARAMS,
        name="halves",
    )(moved[0])
    even_key, even_value = [lax.ppermute(a, "blk", swap) for a in passed]
    early = pl.pallas_call(
        early_kernel,
        out_shape=[
            shape((kv_local, key_rows, query_rows), jnp.float32),
            shape((kv_local, query_rows, HEAD_DIM)),
            shape((kv_local, query_rows, HEAD_DIM)),
            shape((kv_local, key_rows, HEAD_DIM)),
            shape((kv_local, key_rows, HEAD_DIM)),
        ],
        in_specs=[HBM] * 5 + [VMEM] * STEPS,
        out_specs=[VMEM] * 5,
        scratch_shapes=[
            pltpu.VMEM((tokens, width), jnp.bfloat16),
            pltpu.VMEM((tokens, width), jnp.bfloat16),
            pltpu.VMEM(lse.shape, jnp.float32),
            pltpu.SemaphoreType.DMA((3 + 2 * kv_local,)),
        ],
        compiler_params=PARAMS,
        name="early",
    )(query, output, lse, key, value, even_key, first_odd, *moved)
    *far, own, dscore = pl.pallas_call(
        functools.partial(main_kernel, n),
        out_shape=[shape((2 * tokens, kv_width))] * (STEPS - 1)
        + [shape((2 * tokens, kv_width), jnp.float32), shape((kv_local, key_rows, query_rows))],
        in_specs=[VMEM] * (7 + n - 1),
        out_specs=[VMEM] * (STEPS + 1),
        scratch_shapes=[pltpu.VMEM((kv_local, query_rows, HEAD_DIM), jnp.bfloat16)],
        compiler_params=PARAMS,
        name="main",
    )(*early, slices[0], even_value, *received[::-1])
    back = [shifted(far[i - 1], "blk", -i) for i in range(STEPS - 1, 0, -1)]
    dq, *ahead = pl.pallas_call(
        functools.partial(query_kernel, n),
        out_shape=[shape((tokens, width))] + [shape((rows, width))] * len(AHEAD),
        in_specs=[VMEM] * 2,
        out_specs=[VMEM] * (1 + len(AHEAD)),
        compiler_params=PARAMS,
        name="query",
    )(dscore, early[3])
    ahead = [exchange(a, "uly", step) for a, step in zip(ahead, AHEAD)]
    *parts, = pl.pallas_call(
        functools.partial(sum_kernel, n),
        out_shape=[
            shape((rows, 2 * kv_width + (0 if step in AHEAD else width))) for step in range(n)
        ],
        in_specs=[VMEM] * (STEPS + 1),
        out_specs=[VMEM] * n,
        scratch_shapes=[pltpu.VMEM((2 * tokens, kv_width), jnp.bfloat16)],
        compiler_params=PARAMS,
        name="sum",
    )(dq, own, *back)
    if AHEAD:
        parts[AHEAD[-1]] = pl.pallas_call(
            pack_kernel,
            out_shape=shape(parts[AHEAD[-1]].shape),
            in_specs=[VMEM] + [ANY] * len(AHEAD),
            out_specs=VMEM,
            compiler_params=PARAMS,
            name="pack",
        )(parts[AHEAD[-1]], *ahead)
    final = [parts[0]] + [exchange(parts[step], "uly", step) for step in range(1, n)]
    return pl.pallas_call(
        functools.partial(place_kernel, n),
        out_shape=[
            shape((rows, width * n)),
            shape((rows, kv_width * n)),
            shape((rows, kv_width * n)),
        ],
        in_specs=[ANY] * (n + len(AHEAD)),
        out_specs=[HBM] * 3,
        scratch_shapes=[pltpu.SemaphoreType.DMA((n, 3))],
        compiler_params=PARAMS,
        name="place",
    )(*final[::-1], *ahead)


def solution(mesh):
    placed = (
        P("blk", "uly"),
        P("blk", "uly"),
        P("blk", "uly"),
        P("blk", "uly"),
        P(("blk", "uly"), None),
        P("uly", "blk"),
    )
    return jax.shard_map(
        lambda *args: tuple(body(*args)),
        mesh=mesh,
        in_specs=placed,
        out_specs=(P(("blk", "uly"), None), P(("blk", "uly"), None), P(("blk", "uly"), None)),
        check_vma=False,
    )
```

```python
import functools

import jax
import jax.numpy as jnp
from jax import lax
from jax.experimental import pallas as pl
from jax.experimental.pallas import tpu as pltpu
from jax.sharding import PartitionSpec as P

QHEADS = 40
KVHEADS = 8
HEAD_DIM = 128
STEPS = 3
GROUP = QHEADS // KVHEADS
SCALE = HEAD_DIM ** (-0.5)
AHEAD = (1, 2)

VMEM = pl.BlockSpec(memory_space=pltpu.VMEM)
ANY = pl.BlockSpec(memory_space=pl.ANY)
HBM = pl.BlockSpec(memory_space=pltpu.HBM)
PARAMS = pltpu.CompilerParams(vmem_limit_bytes=16 * 1024 * 1024)


def shifted(array, axis, by):
    size = lax.axis_size(axis)
    return lax.ppermute(array, axis, [(i, (i + by) % size) for i in range(size)])


def is_power(n):
    return n & (n - 1) == 0


def partner(me, step, n, back=False):
    if is_power(n):
        return lax.bitwise_xor(me, step)
    return lax.rem(me + (n - step if back else step), n)


def exchange(array, axis, step):
    n = lax.axis_size(axis)
    if is_power(n):
        pairs = [(i, i ^ step) for i in range(n)]
    else:
        pairs = [(i, (i + step) % n) for i in range(n)]
    return lax.ppermute(array, axis, pairs)


def nt(a, b):
    return lax.dot_general(a, b, (((1,), (1,)), ((), ())), preferred_element_type=jnp.float32)


def nn(a, b):
    return lax.dot_general(a, b, (((1,), (0,)), ((), ())), preferred_element_type=jnp.float32)


def tn(a, b):
    return lax.dot_general(a, b, (((0,), (0,)), ((), ())), preferred_element_type=jnp.float32)


def prep_kernel(n, grad, key, value, *refs):
    slices, kv, sems = refs[:n], refs[n], refs[n + 1]
    me = lax.axis_index("uly")
    width = slices[0].shape[1]
    tokens = key.shape[0]
    copies = [
        pltpu.make_async_copy(key, kv.at[pl.ds(0, tokens)], sems.at[n]),
        pltpu.make_async_copy(value, kv.at[pl.ds(tokens, tokens)], sems.at[n + 1]),
    ]
    for step in range(n):
        to = partner(me, step, n) if step else me
        columns = pl.ds(pl.multiple_of(to * width, width), width)
        copies.append(pltpu.make_async_copy(grad.at[:, columns], slices[step], sems.at[step]))
    for copy in copies:
        copy.start()
    for copy in copies:
        copy.wait()


def early_kernel(query, output, lse, kv, near_key, *refs):
    moved, refs = refs[: STEPS - 2], refs[STEPS - 2 :]
    prob, queries, outputs, keys, values = refs
    tokens = query.shape[0]
    kv_local = kv.shape[1] // HEAD_DIM
    for g in range(kv_local):
        cols = pl.ds(g * HEAD_DIM, HEAD_DIM)
        keys[g, pl.ds(0, tokens)] = kv[pl.ds(0, tokens), cols]
        values[g, pl.ds(0, tokens)] = kv[pl.ds(tokens, tokens), cols]
        keys[g, pl.ds(tokens, tokens)] = near_key[:, cols]
        for i in range(2, STEPS):
            part = pl.ds(i * tokens, tokens)
            keys[g, part] = moved[i - 2][pl.ds(0, tokens), cols]
            values[g, part] = moved[i - 2][pl.ds(tokens, tokens), cols]
    for g in range(kv_local):
        for h in range(GROUP):
            head = pl.ds((g * GROUP + h) * HEAD_DIM, HEAD_DIM)
            part = pl.ds(h * tokens, tokens)
            queries[g, part] = query[:, head]
            outputs[g, part] = output[:, head]
        lse_row = jnp.concatenate(
            [lse[pl.ds(g * GROUP + h, 1), :] for h in range(GROUP)], axis=1
        )
        prob[g] = jnp.exp(nt(keys[g], queries[g]) * SCALE - lse_row)


def halves_kernel(own, pair, first, second):
    rows = first.shape[0]
    odd = lax.rem(lax.axis_index("blk"), 2) == 1

    @pl.when(odd)
    def _():
        first[...] = pair[pl.ds(0, rows), :]
        second[...] = pair[pl.ds(rows, rows), :]

    @pl.when(jnp.logical_not(odd))
    def _():
        first[...] = own[pl.ds(0, rows), :]
        second[...] = own[pl.ds(rows, rows), :]


def main_kernel(n, prob, queries, outputs, keys, values, mine, near_value, *refs):
    received = refs[: n - 1][::-1]
    rest = refs[n - 1 :]
    far = rest[: STEPS - 1]
    own, dscore, stacked = rest[STEPS - 1 :]
    me = lax.axis_index("uly")
    rows = mine.shape[0]
    tokens = rows * n
    kv_local = prob.shape[0]
    for step in range(n):
        source = partner(me, step, n, back=True) if step else me
        piece = received[step - 1] if step else mine
        start = pl.multiple_of(source * rows, rows)
        for g in range(kv_local):
            for h in range(GROUP):
                stacked[g, pl.ds(start + h * tokens, rows)] = piece[
                    :, pl.ds((g * GROUP + h) * HEAD_DIM, HEAD_DIM)
                ]
    ones = jnp.ones((8, HEAD_DIM), jnp.bfloat16)
    for g in range(kv_local):
        cols = pl.ds(g * HEAD_DIM, HEAD_DIM)

        v = jnp.concatenate(
            [
                values[g, pl.ds(0, tokens)],
                near_value[:, cols],
                values[g, pl.ds(2 * tokens, (STEPS - 2) * tokens)],
            ],
            axis=0,
        )
        go = stacked[g]
        product = go.astype(jnp.float32) * outputs[g].astype(jnp.float32)
        high = product.astype(jnp.bfloat16)
        low = (product - high.astype(jnp.float32)).astype(jnp.bfloat16)
        delta = (nt(ones, high) + nt(ones, low))[0:1, :]
        p = prob[g]
        ds = (p * (nt(v, go) - delta)).astype(jnp.bfloat16)
        dv = nn(p.astype(jnp.bfloat16), go)
        dk = nn(ds, queries[g]) * SCALE
        dscore[g] = ds
        own[pl.ds(0, tokens), cols] = dk[:tokens]
        own[pl.ds(tokens, tokens), cols] = dv[:tokens]
        for i in range(1, STEPS):
            part = slice(i * tokens, (i + 1) * tokens)
            far[i - 1][pl.ds(0, tokens), cols] = dk[part].astype(jnp.bfloat16)
            far[i - 1][pl.ds(tokens, tokens), cols] = dv[part].astype(jnp.bfloat16)


def query_kernel(n, dscore, keys, out, *sends):
    tokens = out.shape[0]
    rows = tokens // n
    for g in range(dscore.shape[0]):
        dq = (tn(dscore[g], keys[g]) * SCALE).astype(jnp.bfloat16)
        for h in range(GROUP):
            out[:, pl.ds((g * GROUP + h) * HEAD_DIM, HEAD_DIM)] = dq[h * tokens : (h + 1) * tokens]
    me = lax.axis_index("uly")
    for step, send in zip(AHEAD, sends):
        start = pl.multiple_of(partner(me, step, n) * rows, rows)
        send[...] = out[pl.ds(start, rows), :]


def sum_kernel(n, dq, own, *refs):
    back = refs[: STEPS - 1]
    sends, total = refs[STEPS - 1 : -1], refs[-1]
    me = lax.axis_index("uly")
    width = dq.shape[1]
    kv_width = own.shape[1]
    tokens = dq.shape[0]
    rows = tokens // n
    acc = own[...]
    for b in back:
        acc = acc + b[...].astype(jnp.float32)
    total[...] = acc.astype(jnp.bfloat16)
    for step in range(n):
        to = partner(me, step, n) if step else me
        start = pl.multiple_of(to * rows, rows)
        first = 0 if step in AHEAD else width
        if first:
            sends[step][:, pl.ds(0, width)] = dq[pl.ds(start, rows), :]
        sends[step][:, pl.ds(first, kv_width)] = total[pl.ds(start, rows), :]
        sends[step][:, pl.ds(first + kv_width, kv_width)] = total[
            pl.ds(pl.multiple_of(start + tokens, rows), rows), :
        ]


def stash_kernel(*refs):
    half = len(refs) // 2
    for source, target in zip(refs[:half], refs[half:]):
        target[...] = source[...]


def place_kernel(n, *refs):
    parts, refs = refs[:n][::-1], refs[n:]
    ahead, (dq, dk, dv, sems) = refs[: len(AHEAD)], refs[len(AHEAD) :]
    me = lax.axis_index("uly")
    width = dq.shape[1] // n
    kv_width = dk.shape[1] // n
    copies = []
    for step in range(n):
        source = partner(me, step, n, back=True) if step else me
        first = 0 if step in AHEAD else width
        pieces = (
            (dk, parts[step], first, kv_width),
            (dv, parts[step], first + kv_width, kv_width),
            (dq, ahead[AHEAD.index(step)] if step in AHEAD else parts[step], 0, width),
        )
        for i, (out, part, at, size) in enumerate(pieces):
            columns = pl.ds(pl.multiple_of(source * size, size), size)
            copies.append(
                pltpu.make_async_copy(
                    part.at[:, pl.ds(at, size)], out.at[:, columns], sems.at[step, i]
                )
            )
    for copy in copies:
        copy.start()
    for copy in copies:
        copy.wait()


def shape(dims, kind=jnp.bfloat16):
    return jax.ShapeDtypeStruct(dims, kind)


def body(query, key, value, output, grad, lse):
    n = lax.axis_size("uly")
    tokens, width = query.shape
    kv_width = key.shape[1]
    kv_local = kv_width // HEAD_DIM
    rows = grad.shape[0]
    key_rows, query_rows = STEPS * tokens, GROUP * tokens
    far_grad, far_key, far_value = (
        pltpu.with_memory_space_constraint(a, pltpu.HBM) for a in (grad, key, value)
    )
    *slices, kv = pl.pallas_call(
        functools.partial(prep_kernel, n),
        out_shape=[shape((rows, width))] * n + [shape((2 * tokens, kv_width))],
        in_specs=[HBM] * 3,
        out_specs=[ANY] * (n + 1),
        scratch_shapes=[pltpu.SemaphoreType.DMA((n + 2,))],
        compiler_params=PARAMS,
        name="prep",
    )(far_grad, far_key, far_value)
    received = [exchange(slices[step], "uly", step) for step in range(1, n)]
    moved = [shifted(kv, "blk", i) for i in range(2, STEPS)]
    swap = [(i, i ^ 1) for i in range(lax.axis_size("blk"))]
    passed = pl.pallas_call(
        halves_kernel,
        out_shape=[shape((tokens, kv_width))] * 2,
        in_specs=[VMEM] * 2,
        out_specs=[VMEM] * 2,
        compiler_params=PARAMS,
        cost_estimate=pl.CostEstimate(flops=1000000000, bytes_accessed=1000, transcendentals=0),
        name="halves",
    )(kv, moved[0])
    near_key, near_value = [lax.ppermute(a, "blk", swap) for a in passed]
    early = pl.pallas_call(
        early_kernel,
        out_shape=[
            shape((kv_local, key_rows, query_rows), jnp.float32),
            shape((kv_local, query_rows, HEAD_DIM)),
            shape((kv_local, query_rows, HEAD_DIM)),
            shape((kv_local, key_rows, HEAD_DIM)),
            shape((kv_local, key_rows, HEAD_DIM)),
        ],
        in_specs=[VMEM] * (3 + STEPS),
        out_specs=[VMEM] * 5,
        compiler_params=PARAMS,
        name="early",
    )(query, output, lse, kv, near_key, *moved)
    *far, own, dscore = pl.pallas_call(
        functools.partial(main_kernel, n),
        out_shape=[shape((2 * tokens, kv_width))] * (STEPS - 1)
        + [shape((2 * tokens, kv_width), jnp.float32), shape((kv_local, key_rows, query_rows))],
        in_specs=[VMEM] * (7 + n - 1),
        out_specs=[VMEM] * (STEPS + 1),
        scratch_shapes=[pltpu.VMEM((kv_local, query_rows, HEAD_DIM), jnp.bfloat16)],
        compiler_params=PARAMS,
        name="main",
    )(*early, slices[0], near_value, *received[::-1])
    back = [shifted(far[i - 1], "blk", -i) for i in range(STEPS - 1, 0, -1)]
    dq, *ahead = pl.pallas_call(
        functools.partial(query_kernel, n),
        out_shape=[shape((tokens, width))] + [shape((rows, width))] * len(AHEAD),
        in_specs=[VMEM] * 2,
        out_specs=[VMEM] * (1 + len(AHEAD)),
        compiler_params=PARAMS,
        name="query",
    )(dscore, early[3])
    ahead = [exchange(a, "uly", step) for a, step in zip(ahead, AHEAD)]
    *parts, = pl.pallas_call(
        functools.partial(sum_kernel, n),
        out_shape=[
            shape((rows, 2 * kv_width + (0 if step in AHEAD else width))) for step in range(n)
        ],
        in_specs=[VMEM] * (STEPS + 1),
        out_specs=[VMEM] * n,
        scratch_shapes=[pltpu.VMEM((2 * tokens, kv_width), jnp.bfloat16)],
        compiler_params=PARAMS,
        name="sum",
    )(dq, own, *back)
    final = [parts[0]] + [exchange(parts[step], "uly", step) for step in range(1, n)]
    ahead = pl.pallas_call(
        stash_kernel,
        out_shape=[shape((rows, width))] * len(AHEAD),
        in_specs=[VMEM] * len(AHEAD),
        out_specs=[VMEM] * len(AHEAD),
        compiler_params=PARAMS,
        cost_estimate=pl.CostEstimate(flops=300 * 10**6, bytes_accessed=1000, transcendentals=0),
        name="stash",
    )(*ahead)
    return pl.pallas_call(
        functools.partial(place_kernel, n),
        out_shape=[
            shape((rows, width * n)),
            shape((rows, kv_width * n)),
            shape((rows, kv_width * n)),
        ],
        in_specs=[ANY] * (n + len(AHEAD)),
        out_specs=[HBM] * 3,
        scratch_shapes=[pltpu.SemaphoreType.DMA((n, 3))],
        compiler_params=PARAMS,
        name="place",
    )(*final[::-1], *ahead)


def solution(mesh):
    placed = (
        P("blk", "uly"),
        P("blk", "uly"),
        P("blk", "uly"),
        P("blk", "uly"),
        P(("blk", "uly"), None),
        P("uly", "blk"),
    )
    return jax.shard_map(
        lambda *args: tuple(body(*args)),
        mesh=mesh,
        in_specs=placed,
        out_specs=(P(("blk", "uly"), None), P(("blk", "uly"), None), P(("blk", "uly"), None)),
        check_vma=False,
    )
```

```python
import functools

import jax
import jax.numpy as jnp
from jax import lax
from jax.experimental import pallas as pl
from jax.experimental.pallas import tpu as pltpu
from jax.sharding import PartitionSpec as P

QHEADS = 40
KVHEADS = 8
HEAD_DIM = 128
STEPS = 3
GROUP = QHEADS // KVHEADS
SCALE = HEAD_DIM ** (-0.5)
AHEAD = (2, 1)

VMEM = pl.BlockSpec(memory_space=pltpu.VMEM)
ANY = pl.BlockSpec(memory_space=pl.ANY)
HBM = pl.BlockSpec(memory_space=pltpu.HBM)
PARAMS = pltpu.CompilerParams(vmem_limit_bytes=16 * 1024 * 1024)


def shifted(array, axis, by):
    size = lax.axis_size(axis)
    return lax.ppermute(array, axis, [(i, (i + by) % size) for i in range(size)])


def is_power(n):
    return n & (n - 1) == 0


def partner(me, step, n, back=False):
    if is_power(n):
        return lax.bitwise_xor(me, step)
    return lax.rem(me + (n - step if back else step), n)


def exchange(array, axis, step):
    n = lax.axis_size(axis)
    if is_power(n):
        pairs = [(i, i ^ step) for i in range(n)]
    else:
        pairs = [(i, (i + step) % n) for i in range(n)]
    return lax.ppermute(array, axis, pairs)


def nt(a, b):
    return lax.dot_general(a, b, (((1,), (1,)), ((), ())), preferred_element_type=jnp.float32)


def nn(a, b):
    return lax.dot_general(a, b, (((1,), (0,)), ((), ())), preferred_element_type=jnp.float32)


def tn(a, b):
    return lax.dot_general(a, b, (((0,), (0,)), ((), ())), preferred_element_type=jnp.float32)


def prep_kernel(n, grad, key, value, *refs):
    slices, kv, sems = refs[:n], refs[n], refs[n + 1]
    me = lax.axis_index("uly")
    width = slices[0].shape[1]
    tokens = key.shape[0]
    copies = [
        pltpu.make_async_copy(key, kv.at[pl.ds(0, tokens)], sems.at[n]),
        pltpu.make_async_copy(value, kv.at[pl.ds(tokens, tokens)], sems.at[n + 1]),
    ]
    for step in range(n):
        to = partner(me, step, n) if step else me
        columns = pl.ds(pl.multiple_of(to * width, width), width)
        copies.append(pltpu.make_async_copy(grad.at[:, columns], slices[step], sems.at[step]))
    for copy in copies:
        copy.start()
    for copy in copies:
        copy.wait()


def turns(n):
    first = [0, n // 2] if n > 2 else [0]
    return first, [step for step in range(n - 1, 0, -1) if step not in first]


def closing(n):
    return [n - 1] + list(range(1, n - 1))


def early_kernel(n, query, output, lse, kv, near_key, *refs):
    moved, refs = refs[: STEPS - 2], refs[STEPS - 2 :]
    keys, values, sides = refs[0], refs[1], refs[2:]
    me = lax.axis_index("uly")
    tokens = query.shape[0]
    rows = tokens // n
    kv_local = kv.shape[1] // HEAD_DIM
    for g in range(kv_local):
        cols = pl.ds(g * HEAD_DIM, HEAD_DIM)
        keys[g, pl.ds(0, tokens)] = kv[pl.ds(0, tokens), cols]
        values[g, pl.ds(0, tokens)] = kv[pl.ds(tokens, tokens), cols]
        keys[g, pl.ds(tokens, tokens)] = near_key[:, cols]
        for i in range(2, STEPS):
            part = pl.ds(i * tokens, tokens)
            keys[g, part] = moved[i - 2][pl.ds(0, tokens), cols]
            values[g, part] = moved[i - 2][pl.ds(tokens, tokens), cols]
    heads = kv_local * GROUP
    lanes = -(-tokens // 128) * 128
    lse_rows = jnp.concatenate([lse[...], jnp.zeros((-heads % 8, tokens), jnp.float32)], axis=0)
    if lanes > tokens:
        lse_rows = jnp.concatenate(
            [lse_rows, jnp.zeros((lse_rows.shape[0], lanes - tokens), jnp.float32)], axis=1
        )
    for half, steps in enumerate(turns(n)):
        prob, low, queries, outputs = sides[4 * half : 4 * half + 4]
        pieces = []
        for index, step in enumerate(steps):
            source = partner(me, step, n, back=True) if step else me
            start = pl.multiple_of(source * rows, rows)
            pieces.append(pltpu.roll(lse_rows, lax.rem(lanes - start, lanes), 1)[:, :rows])
            for g in range(kv_local):
                for h in range(GROUP):
                    head = pl.ds((g * GROUP + h) * HEAD_DIM, HEAD_DIM)
                    part = pl.ds((index * GROUP + h) * rows, rows)
                    queries[g, part] = query[pl.ds(start, rows), head]
                    outputs[g, part] = output[pl.ds(start, rows), head]
        for g in range(kv_local):
            lse_row = jnp.concatenate(
                [p[g * GROUP + h : g * GROUP + h + 1] for p in pieces for h in range(GROUP)], axis=1
            )
            wide = jnp.exp(nt(keys[g], queries[g]) * SCALE - lse_row)
            prob[g] = wide
            low[g] = wide.astype(jnp.bfloat16)


def halves_kernel(own, pair, first, second):
    rows = first.shape[0]
    odd = lax.rem(lax.axis_index("blk"), 2) == 1

    @pl.when(odd)
    def _():
        first[...] = pair[pl.ds(0, rows), :]
        second[...] = pair[pl.ds(rows, rows), :]

    @pl.when(jnp.logical_not(odd))
    def _():
        first[...] = own[pl.ds(0, rows), :]
        second[...] = own[pl.ds(rows, rows), :]


def tile_grads(prob, low, queries, outputs, values, near_value, pieces, g):
    tokens = near_value.shape[0]
    v = jnp.concatenate(
        [
            values[g, pl.ds(0, tokens)],
            near_value[:, pl.ds(g * HEAD_DIM, HEAD_DIM)],
            values[g, pl.ds(2 * tokens, (STEPS - 2) * tokens)],
        ],
        axis=0,
    )
    go = jnp.concatenate(
        [
            piece[:, pl.ds((g * GROUP + h) * HEAD_DIM, HEAD_DIM)]
            for piece in pieces
            for h in range(GROUP)
        ],
        axis=0,
    )
    product = go.astype(jnp.float32) * outputs[g].astype(jnp.float32)
    delta = jnp.sum(product, axis=1)[None, :]
    ds = (prob[g] * (nt(v, go) - delta)).astype(jnp.bfloat16)
    return ds, nn(ds, queries[g]), nn(low[g], go)


def first_kernel(prob, low, queries, outputs, values, near_value, *refs):
    pieces, (dscore, dk, dv) = refs[:-3], refs[-3:]
    for g in range(prob.shape[0]):
        dscore[g], dk[g], dv[g] = tile_grads(
            prob, low, queries, outputs, values, near_value, pieces, g
        )


def main_kernel(prob, low, queries, outputs, values, near_value, dk_first, dv_first, *refs):
    pieces, (*far, own, dscore) = refs[: -STEPS - 1], refs[-STEPS - 1 :]
    tokens = near_value.shape[0]
    for g in range(prob.shape[0]):
        cols = pl.ds(g * HEAD_DIM, HEAD_DIM)
        dscore[g], dk, dv = tile_grads(
            prob, low, queries, outputs, values, near_value, pieces, g
        )
        dk = (dk + dk_first[g]) * SCALE
        dv = dv + dv_first[g]
        own[pl.ds(0, tokens), cols] = dk[:tokens]
        own[pl.ds(tokens, tokens), cols] = dv[:tokens]
        for i in range(1, STEPS):
            part = slice(i * tokens, (i + 1) * tokens)
            far[i - 1][pl.ds(0, tokens), cols] = dk[part].astype(jnp.bfloat16)
            far[i - 1][pl.ds(tokens, tokens), cols] = dv[part].astype(jnp.bfloat16)


def query_kernel(n, keys, *refs):
    dscores, out, sends = refs[:2], refs[2], refs[3:]
    rows = out.shape[0] // n
    me = lax.axis_index("uly")
    for dscore, steps in zip(dscores, turns(n)):
        for g in range(keys.shape[0]):
            dq = (tn(dscore[g], keys[g]) * SCALE).astype(jnp.bfloat16)
            for index, step in enumerate(steps):
                source = partner(me, step, n, back=True) if step else me
                start = pl.multiple_of(source * rows, rows)
                for h in range(GROUP):
                    first = (index * GROUP + h) * rows
                    out[pl.ds(start, rows), pl.ds((g * GROUP + h) * HEAD_DIM, HEAD_DIM)] = dq[
                        first : first + rows
                    ]
    for step, send in zip(AHEAD, sends):
        start = pl.multiple_of(partner(me, step, n) * rows, rows)
        send[...] = out[pl.ds(start, rows), :]


def sum_kernel(n, dq, own, *refs):
    back = refs[: STEPS - 1]
    sends, total = refs[STEPS - 1 : -1], refs[-1]
    me = lax.axis_index("uly")
    width = dq.shape[1]
    kv_width = own.shape[1]
    tokens = dq.shape[0]
    rows = tokens // n
    acc = own[...]
    for b in back:
        acc = acc + b[...].astype(jnp.float32)
    total[...] = acc.astype(jnp.bfloat16)
    for step in range(n):
        to = partner(me, step, n) if step else me
        start = pl.multiple_of(to * rows, rows)
        first = 0 if step in AHEAD else width
        if first:
            sends[step][:, pl.ds(0, width)] = dq[pl.ds(start, rows), :]
        sends[step][:, pl.ds(first, kv_width)] = total[pl.ds(start, rows), :]
        sends[step][:, pl.ds(first + kv_width, kv_width)] = total[
            pl.ds(pl.multiple_of(start + tokens, rows), rows), :
        ]


def stash_kernel(*refs):
    half = len(refs) // 2
    for source, target in zip(refs[:half], refs[half:]):
        target[...] = source[...]


def place_kernel(n, *refs):
    parts, refs = dict(zip(closing(n) + [0], refs[:n])), refs[n:]
    ahead, (dq, dk, dv, sems) = refs[: len(AHEAD)], refs[len(AHEAD) :]
    me = lax.axis_index("uly")
    width = dq.shape[1] // n
    kv_width = dk.shape[1] // n
    copies = []
    for step in range(n):
        source = partner(me, step, n, back=True) if step else me
        first = 0 if step in AHEAD else width
        pieces = (
            (dk, parts[step], first, kv_width),
            (dv, parts[step], first + kv_width, kv_width),
            (dq, ahead[AHEAD.index(step)] if step in AHEAD else parts[step], 0, width),
        )
        for i, (out, part, at, size) in enumerate(pieces):
            columns = pl.ds(pl.multiple_of(source * size, size), size)
            copies.append(
                pltpu.make_async_copy(
                    part.at[:, pl.ds(at, size)], out.at[:, columns], sems.at[step, i]
                )
            )
    for copy in copies:
        copy.start()
    for copy in copies:
        copy.wait()


def shape(dims, kind=jnp.bfloat16):
    return jax.ShapeDtypeStruct(dims, kind)


def body(query, key, value, output, grad, lse):
    n = lax.axis_size("uly")
    tokens, width = query.shape
    kv_width = key.shape[1]
    kv_local = kv_width // HEAD_DIM
    rows = grad.shape[0]
    key_rows, query_rows = STEPS * tokens, GROUP * tokens
    far_grad, far_key, far_value = (
        pltpu.with_memory_space_constraint(a, pltpu.HBM) for a in (grad, key, value)
    )
    *slices, kv = pl.pallas_call(
        functools.partial(prep_kernel, n),
        out_shape=[shape((rows, width))] * n + [shape((2 * tokens, kv_width))],
        in_specs=[HBM] * 3,
        out_specs=[ANY] * (n + 1),
        scratch_shapes=[pltpu.SemaphoreType.DMA((n + 2,))],
        compiler_params=PARAMS,
        name="prep",
    )(far_grad, far_key, far_value)
    received = [exchange(slices[step], "uly", step) for step in range(1, n)]
    moved = [shifted(kv, "blk", i) for i in range(2, STEPS)]
    swap = [(i, i ^ 1) for i in range(lax.axis_size("blk"))]
    passed = pl.pallas_call(
        halves_kernel,
        out_shape=[shape((tokens, kv_width))] * 2,
        in_specs=[VMEM] * 2,
        out_specs=[VMEM] * 2,
        compiler_params=PARAMS,
        cost_estimate=pl.CostEstimate(flops=1000000000, bytes_accessed=1000, transcendentals=0),
        name="halves",
    )(kv, moved[0])
    near_key, near_value = [lax.ppermute(a, "blk", swap) for a in passed]
    columns = [len(steps) * GROUP * rows for steps in turns(n)]
    keys, values, *sides = pl.pallas_call(
        functools.partial(early_kernel, n),
        out_shape=[shape((kv_local, key_rows, HEAD_DIM))] * 2
        + [
            shape(*dims)
            for c in columns
            for dims in (
                ((kv_local, key_rows, c), jnp.float32),
                ((kv_local, key_rows, c),),
                ((kv_local, c, HEAD_DIM),),
                ((kv_local, c, HEAD_DIM),),
            )
        ],
        in_specs=[VMEM] * (3 + STEPS),
        out_specs=[VMEM] * 10,
        compiler_params=PARAMS,
        name="early",
    )(query, output, lse, kv, near_key, *moved)
    received = [slices[0]] + received
    first, last = ([received[step] for step in steps] for steps in turns(n))
    part = shape((kv_local, key_rows, HEAD_DIM), jnp.float32)
    dscore_first, *parts_first = pl.pallas_call(
        first_kernel,
        out_shape=[shape((kv_local, key_rows, columns[0])), part, part],
        in_specs=[VMEM] * (6 + len(first)),
        out_specs=[VMEM] * 3,
        compiler_params=PARAMS,
        name="first",
    )(*sides[:4], values, near_value, *first)
    *far, own, dscore = pl.pallas_call(
        main_kernel,
        out_shape=[shape((2 * tokens, kv_width))] * (STEPS - 1)
        + [
            shape((2 * tokens, kv_width), jnp.float32),
            shape((kv_local, key_rows, columns[1])),
        ],
        in_specs=[VMEM] * (8 + len(last)),
        out_specs=[VMEM] * (STEPS + 1),
        compiler_params=PARAMS,
        name="main",
    )(*sides[4:], values, near_value, *parts_first, *last)
    back = [shifted(far[i - 1], "blk", -i) for i in range(STEPS - 1, 0, -1)]
    dq, *ahead = pl.pallas_call(
        functools.partial(query_kernel, n),
        out_shape=[shape((tokens, width))] + [shape((rows, width))] * len(AHEAD),
        in_specs=[VMEM] * 3,
        out_specs=[VMEM] * (1 + len(AHEAD)),
        compiler_params=PARAMS,
        name="query",
    )(keys, dscore_first, dscore)
    ahead = [exchange(a, "uly", step) for a, step in zip(ahead, AHEAD)]
    *parts, = pl.pallas_call(
        functools.partial(sum_kernel, n),
        out_shape=[
            shape((rows, 2 * kv_width + (0 if step in AHEAD else width))) for step in range(n)
        ],
        in_specs=[VMEM] * (STEPS + 1),
        out_specs=[VMEM] * n,
        scratch_shapes=[pltpu.VMEM((2 * tokens, kv_width), jnp.bfloat16)],
        compiler_params=PARAMS,
        name="sum",
    )(dq, own, *back)
    final = [parts[0]] + [exchange(parts[step], "uly", step) for step in range(1, n)]
    ahead = pl.pallas_call(
        stash_kernel,
        out_shape=[shape((rows, width))] * len(AHEAD),
        in_specs=[VMEM] * len(AHEAD),
        out_specs=[VMEM] * len(AHEAD),
        compiler_params=PARAMS,
        cost_estimate=pl.CostEstimate(flops=300 * 10**6, bytes_accessed=1000, transcendentals=0),
        name="stash",
    )(*ahead)
    return pl.pallas_call(
        functools.partial(place_kernel, n),
        out_shape=[
            shape((rows, width * n)),
            shape((rows, kv_width * n)),
            shape((rows, kv_width * n)),
        ],
        in_specs=[ANY] * (n + len(AHEAD)),
        out_specs=[HBM] * 3,
        scratch_shapes=[pltpu.SemaphoreType.DMA((n, 3))],
        compiler_params=PARAMS,
        name="place",
    )(*(final[step] for step in closing(n)), final[0], *ahead)


def solution(mesh):
    placed = (
        P("blk", "uly"),
        P("blk", "uly"),
        P("blk", "uly"),
        P("blk", "uly"),
        P(("blk", "uly"), None),
        P("uly", "blk"),
    )
    return jax.shard_map(
        lambda *args: tuple(body(*args)),
        mesh=mesh,
        in_specs=placed,
        out_specs=(P(("blk", "uly"), None), P(("blk", "uly"), None), P(("blk", "uly"), None)),
        check_vma=False,
    )
```

```python
import functools

import jax
import jax.numpy as jnp
from jax import lax
from jax.experimental import pallas as pl
from jax.experimental.pallas import tpu as pltpu
from jax.sharding import PartitionSpec as P

QHEADS = 40
KVHEADS = 8
HEAD_DIM = 128
STEPS = 3
GROUP = QHEADS // KVHEADS
SCALE = HEAD_DIM ** (-0.5)
AHEAD = (2, 1)

VMEM = pl.BlockSpec(memory_space=pltpu.VMEM)
ANY = pl.BlockSpec(memory_space=pl.ANY)
HBM = pl.BlockSpec(memory_space=pltpu.HBM)
PARAMS = pltpu.CompilerParams(vmem_limit_bytes=16 * 1024 * 1024)


def shifted(array, axis, by):
    size = lax.axis_size(axis)
    return lax.ppermute(array, axis, [(i, (i + by) % size) for i in range(size)])


def is_power(n):
    return n & (n - 1) == 0


def partner(me, step, n, back=False):
    if is_power(n):
        return lax.bitwise_xor(me, step)
    return lax.rem(me + (n - step if back else step), n)


def exchange(array, axis, step):
    n = lax.axis_size(axis)
    if is_power(n):
        pairs = [(i, i ^ step) for i in range(n)]
    else:
        pairs = [(i, (i + step) % n) for i in range(n)]
    return lax.ppermute(array, axis, pairs)


def nt(a, b):
    return lax.dot_general(a, b, (((1,), (1,)), ((), ())), preferred_element_type=jnp.float32)


def nn(a, b):
    return lax.dot_general(a, b, (((1,), (0,)), ((), ())), preferred_element_type=jnp.float32)


def tn(a, b):
    return lax.dot_general(a, b, (((0,), (0,)), ((), ())), preferred_element_type=jnp.float32)


def prep_kernel(n, grad, key, value, *refs):
    slices, kv, sems = refs[:n], refs[n], refs[n + 1]
    me = lax.axis_index("uly")
    width = slices[0].shape[1]
    tokens = key.shape[0]
    copies = [
        pltpu.make_async_copy(key, kv.at[pl.ds(0, tokens)], sems.at[n]),
        pltpu.make_async_copy(value, kv.at[pl.ds(tokens, tokens)], sems.at[n + 1]),
    ]
    for step in range(n):
        to = partner(me, step, n) if step else me
        columns = pl.ds(pl.multiple_of(to * width, width), width)
        copies.append(pltpu.make_async_copy(grad.at[:, columns], slices[step], sems.at[step]))
    for copy in copies:
        copy.start()
    for copy in copies:
        copy.wait()


def turns(n):
    first = [0, n // 2] if n > 2 else [0]
    return first, [step for step in range(n - 1, 0, -1) if step not in first]


def closing(n):
    return [n - 1] + list(range(1, n - 1))


def early_kernel(n, query, output, lse, kv, near_key, *refs):
    moved, refs = refs[: STEPS - 2], refs[STEPS - 2 :]
    keys, values, sides = refs[0], refs[1], refs[2:]
    me = lax.axis_index("uly")
    tokens = query.shape[0]
    rows = tokens // n
    kv_local = kv.shape[1] // HEAD_DIM
    for g in range(kv_local):
        cols = pl.ds(g * HEAD_DIM, HEAD_DIM)
        keys[g, pl.ds(0, tokens)] = kv[pl.ds(0, tokens), cols]
        values[g, pl.ds(0, tokens)] = kv[pl.ds(tokens, tokens), cols]
        keys[g, pl.ds(tokens, tokens)] = near_key[:, cols]
        for i in range(2, STEPS):
            part = pl.ds(i * tokens, tokens)
            keys[g, part] = moved[i - 2][pl.ds(0, tokens), cols]
            values[g, part] = moved[i - 2][pl.ds(tokens, tokens), cols]
    heads = kv_local * GROUP
    lanes = -(-tokens // 128) * 128
    lse_rows = jnp.concatenate([lse[...], jnp.zeros((-heads % 8, tokens), jnp.float32)], axis=0)
    if lanes > tokens:
        lse_rows = jnp.concatenate(
            [lse_rows, jnp.zeros((lse_rows.shape[0], lanes - tokens), jnp.float32)], axis=1
        )
    for half, steps in enumerate(turns(n)):
        prob, low, queries, outputs = sides[4 * half : 4 * half + 4]
        pieces = []
        for index, step in enumerate(steps):
            source = partner(me, step, n, back=True) if step else me
            start = pl.multiple_of(source * rows, rows)
            pieces.append(pltpu.roll(lse_rows, lax.rem(lanes - start, lanes), 1)[:, :rows])
            for g in range(kv_local):
                for h in range(GROUP):
                    head = pl.ds((g * GROUP + h) * HEAD_DIM, HEAD_DIM)
                    part = pl.ds((index * GROUP + h) * rows, rows)
                    queries[g, part] = query[pl.ds(start, rows), head]
                    outputs[g, part] = output[pl.ds(start, rows), head]
        for g in range(kv_local):
            lse_row = jnp.concatenate(
                [p[g * GROUP + h : g * GROUP + h + 1] for p in pieces for h in range(GROUP)], axis=1
            )
            wide = jnp.exp(nt(keys[g], queries[g]) * SCALE - lse_row)
            prob[g] = wide
            low[g] = wide.astype(jnp.bfloat16)


def halves_kernel(own, pair, first, second):
    rows = first.shape[0]
    odd = lax.rem(lax.axis_index("blk"), 2) == 1

    @pl.when(odd)
    def _():
        first[...] = pair[pl.ds(0, rows), :]
        second[...] = pair[pl.ds(rows, rows), :]

    @pl.when(jnp.logical_not(odd))
    def _():
        first[...] = own[pl.ds(0, rows), :]
        second[...] = own[pl.ds(rows, rows), :]


def score_grads(prob, outputs, values, near_value, pieces):
    tokens = near_value.shape[0]
    heads = range(prob.shape[0])
    stacked, products = [], []
    for g in heads:
        v = jnp.concatenate(
            [
                values[g, pl.ds(0, tokens)],
                near_value[:, pl.ds(g * HEAD_DIM, HEAD_DIM)],
                values[g, pl.ds(2 * tokens, (STEPS - 2) * tokens)],
            ],
            axis=0,
        )
        go = jnp.concatenate(
            [
                piece[:, pl.ds((g * GROUP + h) * HEAD_DIM, HEAD_DIM)]
                for piece in pieces
                for h in range(GROUP)
            ],
            axis=0,
        )
        stacked.append(go)
        products.append(nt(v, go))
    deltas = [
        jnp.sum(stacked[g].astype(jnp.float32) * outputs[g].astype(jnp.float32), axis=1)[None, :]
        for g in heads
    ]
    scores = [
        (prob[g] * (products[g] - deltas[g])).astype(jnp.bfloat16) for g in heads
    ]
    return stacked, scores


def first_kernel(prob, low, queries, outputs, values, near_value, *refs):
    pieces, (dscore, dk, dv) = refs[:-3], refs[-3:]
    stacked, scores = score_grads(prob, outputs, values, near_value, pieces)
    for g in range(prob.shape[0]):
        dscore[g] = scores[g]
        dk[g] = nn(scores[g], queries[g])
        dv[g] = nn(low[g], stacked[g])


def main_kernel(prob, low, queries, outputs, values, near_value, dk_first, dv_first, *refs):
    pieces, (*far, own, dscore) = refs[: -STEPS - 1], refs[-STEPS - 1 :]
    tokens = near_value.shape[0]
    stacked, scores = score_grads(prob, outputs, values, near_value, pieces)
    for g in range(prob.shape[0]):
        cols = pl.ds(g * HEAD_DIM, HEAD_DIM)
        dscore[g] = scores[g]
        dk = (nn(scores[g], queries[g]) + dk_first[g]) * SCALE
        dv = nn(low[g], stacked[g]) + dv_first[g]
        own[pl.ds(0, tokens), cols] = dk[:tokens]
        own[pl.ds(tokens, tokens), cols] = dv[:tokens]
        for i in range(1, STEPS):
            part = slice(i * tokens, (i + 1) * tokens)
            far[i - 1][pl.ds(0, tokens), cols] = dk[part].astype(jnp.bfloat16)
            far[i - 1][pl.ds(tokens, tokens), cols] = dv[part].astype(jnp.bfloat16)


def query_kernel(n, keys, *refs):
    dscores, out, sends = refs[:2], refs[2], refs[3:]
    rows = out.shape[0] // n
    me = lax.axis_index("uly")
    for dscore, steps in zip(dscores, turns(n)):
        for g in range(keys.shape[0]):
            dq = (tn(dscore[g], keys[g]) * SCALE).astype(jnp.bfloat16)
            for index, step in enumerate(steps):
                source = partner(me, step, n, back=True) if step else me
                start = pl.multiple_of(source * rows, rows)
                for h in range(GROUP):
                    first = (index * GROUP + h) * rows
                    out[pl.ds(start, rows), pl.ds((g * GROUP + h) * HEAD_DIM, HEAD_DIM)] = dq[
                        first : first + rows
                    ]
    for step, send in zip(AHEAD, sends):
        start = pl.multiple_of(partner(me, step, n) * rows, rows)
        send[...] = out[pl.ds(start, rows), :]


def sum_kernel(n, dq, own, *refs):
    back = refs[: STEPS - 1]
    sends, total = refs[STEPS - 1 : -1], refs[-1]
    me = lax.axis_index("uly")
    width = dq.shape[1]
    kv_width = own.shape[1]
    tokens = dq.shape[0]
    rows = tokens // n
    acc = own[...]
    for b in back:
        acc = acc + b[...].astype(jnp.float32)
    total[...] = acc.astype(jnp.bfloat16)
    for step in range(n):
        to = partner(me, step, n) if step else me
        start = pl.multiple_of(to * rows, rows)
        first = 0 if step in AHEAD else width
        if first:
            sends[step][:, pl.ds(0, width)] = dq[pl.ds(start, rows), :]
        sends[step][:, pl.ds(first, kv_width)] = total[pl.ds(start, rows), :]
        sends[step][:, pl.ds(first + kv_width, kv_width)] = total[
            pl.ds(pl.multiple_of(start + tokens, rows), rows), :
        ]


def stash_kernel(*refs):
    half = len(refs) // 2
    for source, target in zip(refs[:half], refs[half:]):
        target[...] = source[...]


def place_kernel(n, *refs):
    parts, refs = dict(zip(closing(n) + [0], refs[:n])), refs[n:]
    ahead, (dq, dk, dv, sems) = refs[: len(AHEAD)], refs[len(AHEAD) :]
    me = lax.axis_index("uly")
    width = dq.shape[1] // n
    kv_width = dk.shape[1] // n
    copies = []
    for step in range(n):
        source = partner(me, step, n, back=True) if step else me
        first = 0 if step in AHEAD else width
        pieces = (
            (dk, parts[step], first, kv_width),
            (dv, parts[step], first + kv_width, kv_width),
            (dq, ahead[AHEAD.index(step)] if step in AHEAD else parts[step], 0, width),
        )
        for i, (out, part, at, size) in enumerate(pieces):
            columns = pl.ds(pl.multiple_of(source * size, size), size)
            copies.append(
                pltpu.make_async_copy(
                    part.at[:, pl.ds(at, size)], out.at[:, columns], sems.at[step, i]
                )
            )
    for copy in copies:
        copy.start()
    for copy in copies:
        copy.wait()


def shape(dims, kind=jnp.bfloat16):
    return jax.ShapeDtypeStruct(dims, kind)


def body(query, key, value, output, grad, lse):
    n = lax.axis_size("uly")
    tokens, width = query.shape
    kv_width = key.shape[1]
    kv_local = kv_width // HEAD_DIM
    rows = grad.shape[0]
    key_rows, query_rows = STEPS * tokens, GROUP * tokens
    far_grad, far_key, far_value = (
        pltpu.with_memory_space_constraint(a, pltpu.HBM) for a in (grad, key, value)
    )
    *slices, kv = pl.pallas_call(
        functools.partial(prep_kernel, n),
        out_shape=[shape((rows, width))] * n + [shape((2 * tokens, kv_width))],
        in_specs=[HBM] * 3,
        out_specs=[ANY] * (n + 1),
        scratch_shapes=[pltpu.SemaphoreType.DMA((n + 2,))],
        compiler_params=PARAMS,
        name="prep",
    )(far_grad, far_key, far_value)
    received = [exchange(slices[step], "uly", step) for step in range(1, n)]
    moved = [shifted(kv, "blk", i) for i in range(2, STEPS)]
    swap = [(i, i ^ 1) for i in range(lax.axis_size("blk"))]
    passed = pl.pallas_call(
        halves_kernel,
        out_shape=[shape((tokens, kv_width))] * 2,
        in_specs=[VMEM] * 2,
        out_specs=[VMEM] * 2,
        compiler_params=PARAMS,
        cost_estimate=pl.CostEstimate(flops=1000000000, bytes_accessed=1000, transcendentals=0),
        name="halves",
    )(kv, moved[0])
    near_key, near_value = [lax.ppermute(a, "blk", swap) for a in passed]
    columns = [len(steps) * GROUP * rows for steps in turns(n)]
    keys, values, *sides = pl.pallas_call(
        functools.partial(early_kernel, n),
        out_shape=[shape((kv_local, key_rows, HEAD_DIM))] * 2
        + [
            shape(*dims)
            for c in columns
            for dims in (
                ((kv_local, key_rows, c), jnp.float32),
                ((kv_local, key_rows, c),),
                ((kv_local, c, HEAD_DIM),),
                ((kv_local, c, HEAD_DIM),),
            )
        ],
        in_specs=[VMEM] * (3 + STEPS),
        out_specs=[VMEM] * 10,
        compiler_params=PARAMS,
        name="early",
    )(query, output, lse, kv, near_key, *moved)
    received = [slices[0]] + received
    first, last = ([received[step] for step in steps] for steps in turns(n))
    part = shape((kv_local, key_rows, HEAD_DIM), jnp.float32)
    dscore_first, *parts_first = pl.pallas_call(
        first_kernel,
        out_shape=[shape((kv_local, key_rows, columns[0])), part, part],
        in_specs=[VMEM] * (6 + len(first)),
        out_specs=[VMEM] * 3,
        compiler_params=PARAMS,
        name="first",
    )(*sides[:4], values, near_value, *first)
    *far, own, dscore = pl.pallas_call(
        main_kernel,
        out_shape=[shape((2 * tokens, kv_width))] * (STEPS - 1)
        + [
            shape((2 * tokens, kv_width), jnp.float32),
            shape((kv_local, key_rows, columns[1])),
        ],
        in_specs=[VMEM] * (8 + len(last)),
        out_specs=[VMEM] * (STEPS + 1),
        compiler_params=PARAMS,
        name="main",
    )(*sides[4:], values, near_value, *parts_first, *last)
    back = [shifted(far[i - 1], "blk", -i) for i in range(STEPS - 1, 0, -1)]
    dq, *ahead = pl.pallas_call(
        functools.partial(query_kernel, n),
        out_shape=[shape((tokens, width))] + [shape((rows, width))] * len(AHEAD),
        in_specs=[VMEM] * 3,
        out_specs=[VMEM] * (1 + len(AHEAD)),
        compiler_params=PARAMS,
        name="query",
    )(keys, dscore_first, dscore)
    ahead = [exchange(a, "uly", step) for a, step in zip(ahead, AHEAD)]
    *parts, = pl.pallas_call(
        functools.partial(sum_kernel, n),
        out_shape=[
            shape((rows, 2 * kv_width + (0 if step in AHEAD else width))) for step in range(n)
        ],
        in_specs=[VMEM] * (STEPS + 1),
        out_specs=[VMEM] * n,
        scratch_shapes=[pltpu.VMEM((2 * tokens, kv_width), jnp.bfloat16)],
        compiler_params=PARAMS,
        name="sum",
    )(dq, own, *back)
    final = [parts[0]] + [exchange(parts[step], "uly", step) for step in range(1, n)]
    ahead = pl.pallas_call(
        stash_kernel,
        out_shape=[shape((rows, width))] * len(AHEAD),
        in_specs=[VMEM] * len(AHEAD),
        out_specs=[VMEM] * len(AHEAD),
        compiler_params=PARAMS,
        cost_estimate=pl.CostEstimate(flops=300 * 10**6, bytes_accessed=1000, transcendentals=0),
        name="stash",
    )(*ahead)
    return pl.pallas_call(
        functools.partial(place_kernel, n),
        out_shape=[
            shape((rows, width * n)),
            shape((rows, kv_width * n)),
            shape((rows, kv_width * n)),
        ],
        in_specs=[ANY] * (n + len(AHEAD)),
        out_specs=[HBM] * 3,
        scratch_shapes=[pltpu.SemaphoreType.DMA((n, 3))],
        compiler_params=PARAMS,
        name="place",
    )(*(final[step] for step in closing(n)), final[0], *ahead)


def solution(mesh):
    placed = (
        P("blk", "uly"),
        P("blk", "uly"),
        P("blk", "uly"),
        P("blk", "uly"),
        P(("blk", "uly"), None),
        P("uly", "blk"),
    )
    return jax.shard_map(
        lambda *args: tuple(body(*args)),
        mesh=mesh,
        in_specs=placed,
        out_specs=(P(("blk", "uly"), None), P(("blk", "uly"), None), P(("blk", "uly"), None)),
        check_vma=False,
    )
```

```python
import functools

import jax
import jax.numpy as jnp
from jax import lax
from jax.experimental import pallas as pl
from jax.experimental.pallas import tpu as pltpu
from jax.sharding import PartitionSpec as P

QHEADS = 40
KVHEADS = 8
HEAD_DIM = 128
STEPS = 3
GROUP = QHEADS // KVHEADS
SCALE = HEAD_DIM ** (-0.5)
AHEAD = (2, 1)

VMEM = pl.BlockSpec(memory_space=pltpu.VMEM)
ANY = pl.BlockSpec(memory_space=pl.ANY)
HBM = pl.BlockSpec(memory_space=pltpu.HBM)
PARAMS = pltpu.CompilerParams(vmem_limit_bytes=16 * 1024 * 1024)


def shifted(array, axis, by):
    size = lax.axis_size(axis)
    return lax.ppermute(array, axis, [(i, (i + by) % size) for i in range(size)])


def is_power(n):
    return n & (n - 1) == 0


def partner(me, step, n, back=False):
    if is_power(n):
        return lax.bitwise_xor(me, step)
    return lax.rem(me + (n - step if back else step), n)


def exchange(array, axis, step):
    n = lax.axis_size(axis)
    if is_power(n):
        pairs = [(i, i ^ step) for i in range(n)]
    else:
        pairs = [(i, (i + step) % n) for i in range(n)]
    return lax.ppermute(array, axis, pairs)


def nt(a, b):
    return lax.dot_general(a, b, (((1,), (1,)), ((), ())), preferred_element_type=jnp.float32)


def nn(a, b):
    return lax.dot_general(a, b, (((1,), (0,)), ((), ())), preferred_element_type=jnp.float32)


def tn(a, b):
    return lax.dot_general(a, b, (((0,), (0,)), ((), ())), preferred_element_type=jnp.float32)


def prep_kernel(n, grad, key, value, *refs):
    slices, kv, sems = refs[:n], refs[n], refs[n + 1]
    me = lax.axis_index("uly")
    width = slices[0].shape[1]
    tokens = key.shape[0]
    copies = [
        pltpu.make_async_copy(key, kv.at[pl.ds(0, tokens)], sems.at[n]),
        pltpu.make_async_copy(value, kv.at[pl.ds(tokens, tokens)], sems.at[n + 1]),
    ]
    for step in range(n):
        to = partner(me, step, n) if step else me
        columns = pl.ds(pl.multiple_of(to * width, width), width)
        copies.append(pltpu.make_async_copy(grad.at[:, columns], slices[step], sems.at[step]))
    for copy in copies:
        copy.start()
    for copy in copies:
        copy.wait()


def turns(n):
    first = [0, n // 2] if n > 2 else [0]
    return first, [step for step in range(n - 1, 0, -1) if step not in first]


def closing(n):
    return [n - 1] + list(range(1, n - 1))


def early_kernel(n, query, output, lse, kv, near_key, *refs):
    moved, refs = refs[: STEPS - 2], refs[STEPS - 2 :]
    keys, values, sides = refs[0], refs[1], refs[2:]
    me = lax.axis_index("uly")
    tokens = query.shape[0]
    rows = tokens // n
    kv_local = kv.shape[1] // HEAD_DIM
    for g in range(kv_local):
        cols = pl.ds(g * HEAD_DIM, HEAD_DIM)
        keys[g, pl.ds(0, tokens)] = kv[pl.ds(0, tokens), cols]
        values[g, pl.ds(0, tokens)] = kv[pl.ds(tokens, tokens), cols]
        keys[g, pl.ds(tokens, tokens)] = near_key[:, cols]
        for i in range(2, STEPS):
            part = pl.ds(i * tokens, tokens)
            keys[g, part] = moved[i - 2][pl.ds(0, tokens), cols]
            values[g, part] = moved[i - 2][pl.ds(tokens, tokens), cols]
    heads = kv_local * GROUP
    lanes = -(-tokens // 128) * 128
    lse_rows = jnp.concatenate([lse[...], jnp.zeros((-heads % 8, tokens), jnp.float32)], axis=0)
    if lanes > tokens:
        lse_rows = jnp.concatenate(
            [lse_rows, jnp.zeros((lse_rows.shape[0], lanes - tokens), jnp.float32)], axis=1
        )
    for half, steps in enumerate(turns(n)):
        prob, low, queries, outputs = sides[4 * half : 4 * half + 4]
        pieces = []
        for index, step in enumerate(steps):
            source = partner(me, step, n, back=True) if step else me
            start = pl.multiple_of(source * rows, rows)
            pieces.append(pltpu.roll(lse_rows, lax.rem(lanes - start, lanes), 1)[:, :rows])
            for g in range(kv_local):
                for h in range(GROUP):
                    head = pl.ds((g * GROUP + h) * HEAD_DIM, HEAD_DIM)
                    part = pl.ds((index * GROUP + h) * rows, rows)
                    queries[g, part] = query[pl.ds(start, rows), head]
                    outputs[g, part] = output[pl.ds(start, rows), head]
        for g in range(kv_local):
            lse_row = jnp.concatenate(
                [p[g * GROUP + h : g * GROUP + h + 1] for p in pieces for h in range(GROUP)], axis=1
            )
            wide = jnp.exp(nt(keys[g], queries[g]) * SCALE - lse_row)
            prob[g] = wide
            low[g] = wide.astype(jnp.bfloat16)


def halves_kernel(own, pair, first, second):
    rows = first.shape[0]
    odd = lax.rem(lax.axis_index("blk"), 2) == 1

    @pl.when(odd)
    def _():
        first[...] = pair[pl.ds(0, rows), :]
        second[...] = pair[pl.ds(rows, rows), :]

    @pl.when(jnp.logical_not(odd))
    def _():
        first[...] = own[pl.ds(0, rows), :]
        second[...] = own[pl.ds(rows, rows), :]


def score_grads(prob, outputs, values, near_value, pieces):
    tokens = near_value.shape[0]
    heads = range(prob.shape[0])
    stacked, products = [], []
    for g in heads:
        v = jnp.concatenate(
            [
                values[g, pl.ds(0, tokens)],
                near_value[:, pl.ds(g * HEAD_DIM, HEAD_DIM)],
                values[g, pl.ds(2 * tokens, (STEPS - 2) * tokens)],
            ],
            axis=0,
        )
        go = jnp.concatenate(
            [
                piece[:, pl.ds((g * GROUP + h) * HEAD_DIM, HEAD_DIM)]
                for piece in pieces
                for h in range(GROUP)
            ],
            axis=0,
        )
        stacked.append(go)
        products.append(nt(v, go))
    deltas = [
        jnp.sum(stacked[g].astype(jnp.float32) * outputs[g].astype(jnp.float32), axis=1)[None, :]
        for g in heads
    ]
    scores = [
        (prob[g] * (products[g] - deltas[g])).astype(jnp.bfloat16) for g in heads
    ]
    return stacked, scores


def first_kernel(prob, low, queries, outputs, values, near_value, keys, *refs):
    pieces, (dq, dk, dv) = refs[:-3], refs[-3:]
    stacked, scores = score_grads(prob, outputs, values, near_value, pieces)
    rows = pieces[0].shape[0]
    for g in range(prob.shape[0]):
        dk[g] = nn(scores[g], queries[g])
        dv[g] = nn(low[g], stacked[g])
        query_rows = (tn(scores[g], keys[g]) * SCALE).astype(jnp.bfloat16)
        for index in range(len(pieces)):
            for h in range(GROUP):
                start = (index * GROUP + h) * rows
                dq[pl.ds(index * rows, rows), pl.ds((g * GROUP + h) * HEAD_DIM, HEAD_DIM)] = (
                    query_rows[start : start + rows]
                )


def main_kernel(prob, low, queries, outputs, values, near_value, dk_first, dv_first, *refs):
    pieces, (*far, own, dscore) = refs[: -STEPS - 1], refs[-STEPS - 1 :]
    tokens = near_value.shape[0]
    stacked, scores = score_grads(prob, outputs, values, near_value, pieces)
    for g in range(prob.shape[0]):
        cols = pl.ds(g * HEAD_DIM, HEAD_DIM)
        dscore[g] = scores[g]
        dk = (nn(scores[g], queries[g]) + dk_first[g]) * SCALE
        dv = nn(low[g], stacked[g]) + dv_first[g]
        own[pl.ds(0, tokens), cols] = dk[:tokens]
        own[pl.ds(tokens, tokens), cols] = dv[:tokens]
        for i in range(1, STEPS):
            part = slice(i * tokens, (i + 1) * tokens)
            far[i - 1][pl.ds(0, tokens), cols] = dk[part].astype(jnp.bfloat16)
            far[i - 1][pl.ds(tokens, tokens), cols] = dv[part].astype(jnp.bfloat16)


def query_kernel(n, keys, dq_first, dscore, out, *sends):
    rows = out.shape[0] // n
    me = lax.axis_index("uly")
    first, last = turns(n)
    for index, step in enumerate(first):
        source = partner(me, step, n, back=True) if step else me
        out[pl.ds(pl.multiple_of(source * rows, rows), rows), :] = dq_first[
            pl.ds(index * rows, rows), :
        ]
    for g in range(keys.shape[0]):
        dq = (tn(dscore[g], keys[g]) * SCALE).astype(jnp.bfloat16)
        for index, step in enumerate(last):
            start = pl.multiple_of(partner(me, step, n, back=True) * rows, rows)
            for h in range(GROUP):
                at = (index * GROUP + h) * rows
                out[pl.ds(start, rows), pl.ds((g * GROUP + h) * HEAD_DIM, HEAD_DIM)] = dq[
                    at : at + rows
                ]
    for step, send in zip(AHEAD, sends):
        start = pl.multiple_of(partner(me, step, n) * rows, rows)
        send[...] = out[pl.ds(start, rows), :]


def sum_kernel(n, dq, own, *refs):
    back = refs[: STEPS - 1]
    sends, total = refs[STEPS - 1 : -1], refs[-1]
    me = lax.axis_index("uly")
    width = dq.shape[1]
    kv_width = own.shape[1]
    tokens = dq.shape[0]
    rows = tokens // n
    acc = own[...]
    for b in back:
        acc = acc + b[...].astype(jnp.float32)
    total[...] = acc.astype(jnp.bfloat16)
    for step in range(n):
        to = partner(me, step, n) if step else me
        start = pl.multiple_of(to * rows, rows)
        first = 0 if step in AHEAD else width
        if first:
            sends[step][:, pl.ds(0, width)] = dq[pl.ds(start, rows), :]
        sends[step][:, pl.ds(first, kv_width)] = total[pl.ds(start, rows), :]
        sends[step][:, pl.ds(first + kv_width, kv_width)] = total[
            pl.ds(pl.multiple_of(start + tokens, rows), rows), :
        ]


def stash_kernel(*refs):
    half = len(refs) // 2
    for source, target in zip(refs[:half], refs[half:]):
        target[...] = source[...]


def place_kernel(n, *refs):
    parts, refs = dict(zip(closing(n) + [0], refs[:n])), refs[n:]
    ahead, (dq, dk, dv, sems) = refs[: len(AHEAD)], refs[len(AHEAD) :]
    me = lax.axis_index("uly")
    width = dq.shape[1] // n
    kv_width = dk.shape[1] // n
    copies = []
    for step in range(n):
        source = partner(me, step, n, back=True) if step else me
        first = 0 if step in AHEAD else width
        pieces = (
            (dk, parts[step], first, kv_width),
            (dv, parts[step], first + kv_width, kv_width),
            (dq, ahead[AHEAD.index(step)] if step in AHEAD else parts[step], 0, width),
        )
        for i, (out, part, at, size) in enumerate(pieces):
            columns = pl.ds(pl.multiple_of(source * size, size), size)
            copies.append(
                pltpu.make_async_copy(
                    part.at[:, pl.ds(at, size)], out.at[:, columns], sems.at[step, i]
                )
            )
    for copy in copies:
        copy.start()
    for copy in copies:
        copy.wait()


def shape(dims, kind=jnp.bfloat16):
    return jax.ShapeDtypeStruct(dims, kind)


def body(query, key, value, output, grad, lse):
    n = lax.axis_size("uly")
    tokens, width = query.shape
    kv_width = key.shape[1]
    kv_local = kv_width // HEAD_DIM
    rows = grad.shape[0]
    key_rows, query_rows = STEPS * tokens, GROUP * tokens
    far_grad, far_key, far_value = (
        pltpu.with_memory_space_constraint(a, pltpu.HBM) for a in (grad, key, value)
    )
    *slices, kv = pl.pallas_call(
        functools.partial(prep_kernel, n),
        out_shape=[shape((rows, width))] * n + [shape((2 * tokens, kv_width))],
        in_specs=[HBM] * 3,
        out_specs=[ANY] * (n + 1),
        scratch_shapes=[pltpu.SemaphoreType.DMA((n + 2,))],
        compiler_params=PARAMS,
        name="prep",
    )(far_grad, far_key, far_value)
    received = [exchange(slices[step], "uly", step) for step in range(1, n)]
    moved = [shifted(kv, "blk", i) for i in range(2, STEPS)]
    swap = [(i, i ^ 1) for i in range(lax.axis_size("blk"))]
    passed = pl.pallas_call(
        halves_kernel,
        out_shape=[shape((tokens, kv_width))] * 2,
        in_specs=[VMEM] * 2,
        out_specs=[VMEM] * 2,
        compiler_params=PARAMS,
        cost_estimate=pl.CostEstimate(flops=1000000000, bytes_accessed=1000, transcendentals=0),
        name="halves",
    )(kv, moved[0])
    near_key, near_value = [lax.ppermute(a, "blk", swap) for a in passed]
    columns = [len(steps) * GROUP * rows for steps in turns(n)]
    keys, values, *sides = pl.pallas_call(
        functools.partial(early_kernel, n),
        out_shape=[shape((kv_local, key_rows, HEAD_DIM))] * 2
        + [
            shape(*dims)
            for c in columns
            for dims in (
                ((kv_local, key_rows, c), jnp.float32),
                ((kv_local, key_rows, c),),
                ((kv_local, c, HEAD_DIM),),
                ((kv_local, c, HEAD_DIM),),
            )
        ],
        in_specs=[VMEM] * (3 + STEPS),
        out_specs=[VMEM] * 10,
        compiler_params=PARAMS,
        name="early",
    )(query, output, lse, kv, near_key, *moved)
    received = [slices[0]] + received
    first, last = ([received[step] for step in steps] for steps in turns(n))
    part = shape((kv_local, key_rows, HEAD_DIM), jnp.float32)
    dq_first, *parts_first = pl.pallas_call(
        first_kernel,
        out_shape=[shape((len(first) * rows, width)), part, part],
        in_specs=[VMEM] * (7 + len(first)),
        out_specs=[VMEM] * 3,
        compiler_params=PARAMS,
        name="first",
    )(*sides[:4], values, near_value, keys, *first)
    *far, own, dscore = pl.pallas_call(
        main_kernel,
        out_shape=[shape((2 * tokens, kv_width))] * (STEPS - 1)
        + [
            shape((2 * tokens, kv_width), jnp.float32),
            shape((kv_local, key_rows, columns[1])),
        ],
        in_specs=[VMEM] * (8 + len(last)),
        out_specs=[VMEM] * (STEPS + 1),
        compiler_params=PARAMS,
        name="main",
    )(*sides[4:], values, near_value, *parts_first, *last)
    back = [shifted(far[i - 1], "blk", -i) for i in range(STEPS - 1, 0, -1)]
    dq, *ahead = pl.pallas_call(
        functools.partial(query_kernel, n),
        out_shape=[shape((tokens, width))] + [shape((rows, width))] * len(AHEAD),
        in_specs=[VMEM] * 3,
        out_specs=[VMEM] * (1 + len(AHEAD)),
        compiler_params=PARAMS,
        name="query",
    )(keys, dq_first, dscore)
    ahead = [exchange(a, "uly", step) for a, step in zip(ahead, AHEAD)]
    *parts, = pl.pallas_call(
        functools.partial(sum_kernel, n),
        out_shape=[
            shape((rows, 2 * kv_width + (0 if step in AHEAD else width))) for step in range(n)
        ],
        in_specs=[VMEM] * (STEPS + 1),
        out_specs=[VMEM] * n,
        scratch_shapes=[pltpu.VMEM((2 * tokens, kv_width), jnp.bfloat16)],
        compiler_params=PARAMS,
        name="sum",
    )(dq, own, *back)
    final = [parts[0]] + [exchange(parts[step], "uly", step) for step in range(1, n)]
    ahead = pl.pallas_call(
        stash_kernel,
        out_shape=[shape((rows, width))] * len(AHEAD),
        in_specs=[VMEM] * len(AHEAD),
        out_specs=[VMEM] * len(AHEAD),
        compiler_params=PARAMS,
        cost_estimate=pl.CostEstimate(flops=300 * 10**6, bytes_accessed=1000, transcendentals=0),
        name="stash",
    )(*ahead)
    return pl.pallas_call(
        functools.partial(place_kernel, n),
        out_shape=[
            shape((rows, width * n)),
            shape((rows, kv_width * n)),
            shape((rows, kv_width * n)),
        ],
        in_specs=[ANY] * (n + len(AHEAD)),
        out_specs=[HBM] * 3,
        scratch_shapes=[pltpu.SemaphoreType.DMA((n, 3))],
        compiler_params=PARAMS,
        name="place",
    )(*(final[step] for step in closing(n)), final[0], *ahead)


def solution(mesh):
    placed = (
        P("blk", "uly"),
        P("blk", "uly"),
        P("blk", "uly"),
        P("blk", "uly"),
        P(("blk", "uly"), None),
        P("uly", "blk"),
    )
    return jax.shard_map(
        lambda *args: tuple(body(*args)),
        mesh=mesh,
        in_specs=placed,
        out_specs=(P(("blk", "uly"), None), P(("blk", "uly"), None), P(("blk", "uly"), None)),
        check_vma=False,
    )
```

```python
import functools

import jax
import jax.numpy as jnp
from jax import lax
from jax.experimental import pallas as pl
from jax.experimental.pallas import tpu as pltpu
from jax.sharding import PartitionSpec as P

QHEADS = 40
KVHEADS = 8
HEAD_DIM = 128
STEPS = 3
GROUP = QHEADS // KVHEADS
SCALE = HEAD_DIM ** (-0.5)
AHEAD = (2, 1)

VMEM = pl.BlockSpec(memory_space=pltpu.VMEM)
ANY = pl.BlockSpec(memory_space=pl.ANY)
HBM = pl.BlockSpec(memory_space=pltpu.HBM)
PARAMS = pltpu.CompilerParams(vmem_limit_bytes=16 * 1024 * 1024)


def shifted(array, axis, by):
    size = lax.axis_size(axis)
    return lax.ppermute(array, axis, [(i, (i + by) % size) for i in range(size)])


def is_power(n):
    return n & (n - 1) == 0


def partner(me, step, n, back=False):
    if is_power(n):
        return lax.bitwise_xor(me, step)
    return lax.rem(me + (n - step if back else step), n)


def exchange(array, axis, step):
    n = lax.axis_size(axis)
    if is_power(n):
        pairs = [(i, i ^ step) for i in range(n)]
    else:
        pairs = [(i, (i + step) % n) for i in range(n)]
    return lax.ppermute(array, axis, pairs)


def nt(a, b):
    return lax.dot_general(a, b, (((1,), (1,)), ((), ())), preferred_element_type=jnp.float32)


def nn(a, b):
    return lax.dot_general(a, b, (((1,), (0,)), ((), ())), preferred_element_type=jnp.float32)


def tn(a, b):
    return lax.dot_general(a, b, (((0,), (0,)), ((), ())), preferred_element_type=jnp.float32)


def prep_kernel(n, grad, key, value, *refs):
    slices, kv, sems = refs[:n], refs[n], refs[n + 1]
    me = lax.axis_index("uly")
    width = slices[0].shape[1]
    tokens = key.shape[0]
    copies = [
        pltpu.make_async_copy(key, kv.at[pl.ds(0, tokens)], sems.at[n]),
        pltpu.make_async_copy(value, kv.at[pl.ds(tokens, tokens)], sems.at[n + 1]),
    ]
    for step in range(n):
        to = partner(me, step, n) if step else me
        columns = pl.ds(pl.multiple_of(to * width, width), width)
        copies.append(pltpu.make_async_copy(grad.at[:, columns], slices[step], sems.at[step]))
    for copy in copies:
        copy.start()
    for copy in copies:
        copy.wait()


def turns(n):
    first = [0, n // 2] if n > 2 else [0]
    return first, [step for step in range(n - 1, 0, -1) if step not in first]


def ready(n):
    return [step for step in AHEAD if is_power(n) and step in turns(n)[0]]


def closing(n):
    return [n - 1] + list(range(1, n - 1))


def early_kernel(n, query, output, lse, kv, near_key, *refs):
    moved, refs = refs[: STEPS - 2], refs[STEPS - 2 :]
    keys, values, sides = refs[0], refs[1], refs[2:]
    me = lax.axis_index("uly")
    tokens = query.shape[0]
    rows = tokens // n
    kv_local = kv.shape[1] // HEAD_DIM
    for g in range(kv_local):
        cols = pl.ds(g * HEAD_DIM, HEAD_DIM)
        keys[g, pl.ds(0, tokens)] = kv[pl.ds(0, tokens), cols]
        values[g, pl.ds(0, tokens)] = kv[pl.ds(tokens, tokens), cols]
        keys[g, pl.ds(tokens, tokens)] = near_key[:, cols]
        for i in range(2, STEPS):
            part = pl.ds(i * tokens, tokens)
            keys[g, part] = moved[i - 2][pl.ds(0, tokens), cols]
            values[g, part] = moved[i - 2][pl.ds(tokens, tokens), cols]
    heads = kv_local * GROUP
    lanes = -(-tokens // 128) * 128
    lse_rows = jnp.concatenate([lse[...], jnp.zeros((-heads % 8, tokens), jnp.float32)], axis=0)
    if lanes > tokens:
        lse_rows = jnp.concatenate(
            [lse_rows, jnp.zeros((lse_rows.shape[0], lanes - tokens), jnp.float32)], axis=1
        )
    for half, steps in enumerate(turns(n)):
        prob, low, queries, outputs = sides[4 * half : 4 * half + 4]
        pieces = []
        for index, step in enumerate(steps):
            source = partner(me, step, n, back=True) if step else me
            start = pl.multiple_of(source * rows, rows)
            pieces.append(pltpu.roll(lse_rows, lax.rem(lanes - start, lanes), 1)[:, :rows])
            for g in range(kv_local):
                for h in range(GROUP):
                    head = pl.ds((g * GROUP + h) * HEAD_DIM, HEAD_DIM)
                    part = pl.ds((index * GROUP + h) * rows, rows)
                    queries[g, part] = query[pl.ds(start, rows), head]
                    outputs[g, part] = output[pl.ds(start, rows), head]
        for g in range(kv_local):
            lse_row = jnp.concatenate(
                [p[g * GROUP + h : g * GROUP + h + 1] for p in pieces for h in range(GROUP)], axis=1
            )
            wide = jnp.exp(nt(keys[g], queries[g]) * SCALE - lse_row)
            prob[g] = wide
            low[g] = wide.astype(jnp.bfloat16)


def halves_kernel(own, pair, first, second):
    rows = first.shape[0]
    odd = lax.rem(lax.axis_index("blk"), 2) == 1

    @pl.when(odd)
    def _():
        first[...] = pair[pl.ds(0, rows), :]
        second[...] = pair[pl.ds(rows, rows), :]

    @pl.when(jnp.logical_not(odd))
    def _():
        first[...] = own[pl.ds(0, rows), :]
        second[...] = own[pl.ds(rows, rows), :]


def score_grads(prob, outputs, values, near_value, pieces):
    tokens = near_value.shape[0]
    heads = range(prob.shape[0])
    stacked, products = [], []
    for g in heads:
        v = jnp.concatenate(
            [
                values[g, pl.ds(0, tokens)],
                near_value[:, pl.ds(g * HEAD_DIM, HEAD_DIM)],
                values[g, pl.ds(2 * tokens, (STEPS - 2) * tokens)],
            ],
            axis=0,
        )
        go = jnp.concatenate(
            [
                piece[:, pl.ds((g * GROUP + h) * HEAD_DIM, HEAD_DIM)]
                for piece in pieces
                for h in range(GROUP)
            ],
            axis=0,
        )
        stacked.append(go)
        products.append(nt(v, go))
    deltas = [
        jnp.sum(stacked[g].astype(jnp.float32) * outputs[g].astype(jnp.float32), axis=1)[None, :]
        for g in heads
    ]
    scores = [
        (prob[g] * (products[g] - deltas[g])).astype(jnp.bfloat16) for g in heads
    ]
    return stacked, scores


def first_kernel(n, prob, low, queries, outputs, values, near_value, keys, *refs):
    steps = turns(n)[0]
    pieces, (dq, dk, dv, *sends) = refs[: len(steps)], refs[len(steps) :]
    stacked, scores = score_grads(prob, outputs, values, near_value, pieces)
    rows = pieces[0].shape[0]
    for g in range(prob.shape[0]):
        dk[g] = nn(scores[g], queries[g])
        dv[g] = nn(low[g], stacked[g])
        query_rows = (tn(scores[g], keys[g]) * SCALE).astype(jnp.bfloat16)
        for index in range(len(pieces)):
            for h in range(GROUP):
                start = (index * GROUP + h) * rows
                dq[pl.ds(index * rows, rows), pl.ds((g * GROUP + h) * HEAD_DIM, HEAD_DIM)] = (
                    query_rows[start : start + rows]
                )
    for step, send in zip(ready(n), sends):
        send[...] = dq[pl.ds(steps.index(step) * rows, rows), :]


def main_kernel(prob, low, queries, outputs, values, near_value, dk_first, dv_first, *refs):
    pieces, (*far, own, dscore) = refs[: -STEPS - 1], refs[-STEPS - 1 :]
    tokens = near_value.shape[0]
    stacked, scores = score_grads(prob, outputs, values, near_value, pieces)
    for g in range(prob.shape[0]):
        cols = pl.ds(g * HEAD_DIM, HEAD_DIM)
        dscore[g] = scores[g]
        dk = (nn(scores[g], queries[g]) + dk_first[g]) * SCALE
        dv = nn(low[g], stacked[g]) + dv_first[g]
        own[pl.ds(0, tokens), cols] = dk[:tokens]
        own[pl.ds(tokens, tokens), cols] = dv[:tokens]
        for i in range(1, STEPS):
            part = slice(i * tokens, (i + 1) * tokens)
            far[i - 1][pl.ds(0, tokens), cols] = dk[part].astype(jnp.bfloat16)
            far[i - 1][pl.ds(tokens, tokens), cols] = dv[part].astype(jnp.bfloat16)


def query_kernel(n, keys, dq_first, dscore, out, *sends):
    rows = out.shape[0] // n
    me = lax.axis_index("uly")
    first, last = turns(n)
    for index, step in enumerate(first):
        source = partner(me, step, n, back=True) if step else me
        out[pl.ds(pl.multiple_of(source * rows, rows), rows), :] = dq_first[
            pl.ds(index * rows, rows), :
        ]
    for g in range(keys.shape[0]):
        dq = (tn(dscore[g], keys[g]) * SCALE).astype(jnp.bfloat16)
        for index, step in enumerate(last):
            start = pl.multiple_of(partner(me, step, n, back=True) * rows, rows)
            for h in range(GROUP):
                at = (index * GROUP + h) * rows
                out[pl.ds(start, rows), pl.ds((g * GROUP + h) * HEAD_DIM, HEAD_DIM)] = dq[
                    at : at + rows
                ]
    for step, send in zip([step for step in AHEAD if step not in ready(n)], sends):
        start = pl.multiple_of(partner(me, step, n) * rows, rows)
        send[...] = out[pl.ds(start, rows), :]


def sum_kernel(n, dq, own, *refs):
    back = refs[: STEPS - 1]
    sends, total = refs[STEPS - 1 : -1], refs[-1]
    me = lax.axis_index("uly")
    width = dq.shape[1]
    kv_width = own.shape[1]
    tokens = dq.shape[0]
    rows = tokens // n
    acc = own[...]
    for b in back:
        acc = acc + b[...].astype(jnp.float32)
    total[...] = acc.astype(jnp.bfloat16)
    for step in range(n):
        to = partner(me, step, n) if step else me
        start = pl.multiple_of(to * rows, rows)
        first = 0 if step in AHEAD else width
        if first:
            sends[step][:, pl.ds(0, width)] = dq[pl.ds(start, rows), :]
        sends[step][:, pl.ds(first, kv_width)] = total[pl.ds(start, rows), :]
        sends[step][:, pl.ds(first + kv_width, kv_width)] = total[
            pl.ds(pl.multiple_of(start + tokens, rows), rows), :
        ]


def stash_kernel(*refs):
    half = len(refs) // 2
    for source, target in zip(refs[:half], refs[half:]):
        target[...] = source[...]


def place_kernel(n, *refs):
    parts, refs = dict(zip(closing(n) + [0], refs[:n])), refs[n:]
    ahead, (dq, dk, dv, sems) = refs[: len(AHEAD)], refs[len(AHEAD) :]
    me = lax.axis_index("uly")
    width = dq.shape[1] // n
    kv_width = dk.shape[1] // n
    copies = []
    for step in range(n):
        source = partner(me, step, n, back=True) if step else me
        first = 0 if step in AHEAD else width
        pieces = (
            (dk, parts[step], first, kv_width),
            (dv, parts[step], first + kv_width, kv_width),
            (dq, ahead[AHEAD.index(step)] if step in AHEAD else parts[step], 0, width),
        )
        for i, (out, part, at, size) in enumerate(pieces):
            columns = pl.ds(pl.multiple_of(source * size, size), size)
            copies.append(
                pltpu.make_async_copy(
                    part.at[:, pl.ds(at, size)], out.at[:, columns], sems.at[step, i]
                )
            )
    for copy in copies:
        copy.start()
    for copy in copies:
        copy.wait()


def shape(dims, kind=jnp.bfloat16):
    return jax.ShapeDtypeStruct(dims, kind)


def body(query, key, value, output, grad, lse):
    n = lax.axis_size("uly")
    tokens, width = query.shape
    kv_width = key.shape[1]
    kv_local = kv_width // HEAD_DIM
    rows = grad.shape[0]
    key_rows, query_rows = STEPS * tokens, GROUP * tokens
    far_grad, far_key, far_value = (
        pltpu.with_memory_space_constraint(a, pltpu.HBM) for a in (grad, key, value)
    )
    *slices, kv = pl.pallas_call(
        functools.partial(prep_kernel, n),
        out_shape=[shape((rows, width))] * n + [shape((2 * tokens, kv_width))],
        in_specs=[HBM] * 3,
        out_specs=[ANY] * (n + 1),
        scratch_shapes=[pltpu.SemaphoreType.DMA((n + 2,))],
        compiler_params=PARAMS,
        name="prep",
    )(far_grad, far_key, far_value)
    received = [exchange(slices[step], "uly", step) for step in range(1, n)]
    moved = [shifted(kv, "blk", i) for i in range(2, STEPS)]
    swap = [(i, i ^ 1) for i in range(lax.axis_size("blk"))]
    passed = pl.pallas_call(
        halves_kernel,
        out_shape=[shape((tokens, kv_width))] * 2,
        in_specs=[VMEM] * 2,
        out_specs=[VMEM] * 2,
        compiler_params=PARAMS,
        cost_estimate=pl.CostEstimate(flops=1000000000, bytes_accessed=1000, transcendentals=0),
        name="halves",
    )(kv, moved[0])
    near_key, near_value = [lax.ppermute(a, "blk", swap) for a in passed]
    columns = [len(steps) * GROUP * rows for steps in turns(n)]
    keys, values, *sides = pl.pallas_call(
        functools.partial(early_kernel, n),
        out_shape=[shape((kv_local, key_rows, HEAD_DIM))] * 2
        + [
            shape(*dims)
            for c in columns
            for dims in (
                ((kv_local, key_rows, c), jnp.float32),
                ((kv_local, key_rows, c),),
                ((kv_local, c, HEAD_DIM),),
                ((kv_local, c, HEAD_DIM),),
            )
        ],
        in_specs=[VMEM] * (3 + STEPS),
        out_specs=[VMEM] * 10,
        compiler_params=PARAMS,
        name="early",
    )(query, output, lse, kv, near_key, *moved)
    received = [slices[0]] + received
    first, last = ([received[step] for step in steps] for steps in turns(n))
    part = shape((kv_local, key_rows, HEAD_DIM), jnp.float32)
    dq_first, *parts_first = pl.pallas_call(
        functools.partial(first_kernel, n),
        out_shape=[shape((len(first) * rows, width)), part, part]
        + [shape((rows, width))] * len(ready(n)),
        in_specs=[VMEM] * (7 + len(first)),
        out_specs=[VMEM] * (3 + len(ready(n))),
        compiler_params=PARAMS,
        name="first",
    )(*sides[:4], values, near_value, keys, *first)
    *far, own, dscore = pl.pallas_call(
        main_kernel,
        out_shape=[shape((2 * tokens, kv_width))] * (STEPS - 1)
        + [
            shape((2 * tokens, kv_width), jnp.float32),
            shape((kv_local, key_rows, columns[1])),
        ],
        in_specs=[VMEM] * (8 + len(last)),
        out_specs=[VMEM] * (STEPS + 1),
        compiler_params=PARAMS,
        name="main",
    )(*sides[4:], values, near_value, *parts_first[:2], *last)
    back = [shifted(far[i - 1], "blk", -i) for i in range(STEPS - 1, 0, -1)]
    dq, *ahead = pl.pallas_call(
        functools.partial(query_kernel, n),
        out_shape=[shape((tokens, width))] + [shape((rows, width))] * (len(AHEAD) - len(ready(n))),
        in_specs=[VMEM] * 3,
        out_specs=[VMEM] * (1 + len(AHEAD) - len(ready(n))),
        compiler_params=PARAMS,
        name="query",
    )(keys, dq_first, dscore)
    early_sends, later_sends = iter(parts_first[2:]), iter(ahead)
    ahead = [
        exchange(next(early_sends if step in ready(n) else later_sends), "uly", step)
        for step in AHEAD
    ]
    *parts, = pl.pallas_call(
        functools.partial(sum_kernel, n),
        out_shape=[
            shape((rows, 2 * kv_width + (0 if step in AHEAD else width))) for step in range(n)
        ],
        in_specs=[VMEM] * (STEPS + 1),
        out_specs=[VMEM] * n,
        scratch_shapes=[pltpu.VMEM((2 * tokens, kv_width), jnp.bfloat16)],
        compiler_params=PARAMS,
        name="sum",
    )(dq, own, *back)
    final = [parts[0]] + [exchange(parts[step], "uly", step) for step in range(1, n)]
    ahead = pl.pallas_call(
        stash_kernel,
        out_shape=[shape((rows, width))] * len(AHEAD),
        in_specs=[VMEM] * len(AHEAD),
        out_specs=[VMEM] * len(AHEAD),
        compiler_params=PARAMS,
        cost_estimate=pl.CostEstimate(flops=300 * 10**6, bytes_accessed=1000, transcendentals=0),
        name="stash",
    )(*ahead)
    return pl.pallas_call(
        functools.partial(place_kernel, n),
        out_shape=[
            shape((rows, width * n)),
            shape((rows, kv_width * n)),
            shape((rows, kv_width * n)),
        ],
        in_specs=[ANY] * (n + len(AHEAD)),
        out_specs=[HBM] * 3,
        scratch_shapes=[pltpu.SemaphoreType.DMA((n, 3))],
        compiler_params=PARAMS,
        name="place",
    )(*(final[step] for step in closing(n)), final[0], *ahead)


def solution(mesh):
    placed = (
        P("blk", "uly"),
        P("blk", "uly"),
        P("blk", "uly"),
        P("blk", "uly"),
        P(("blk", "uly"), None),
        P("uly", "blk"),
    )
    return jax.shard_map(
        lambda *args: tuple(body(*args)),
        mesh=mesh,
        in_specs=placed,
        out_specs=(P(("blk", "uly"), None), P(("blk", "uly"), None), P(("blk", "uly"), None)),
        check_vma=False,
    )
```

```python
import functools

import jax
import jax.numpy as jnp
from jax import lax
from jax.experimental import pallas as pl
from jax.experimental.pallas import tpu as pltpu
from jax.sharding import PartitionSpec as P

QHEADS = 40
KVHEADS = 8
HEAD_DIM = 128
STEPS = 3
GROUP = QHEADS // KVHEADS
SCALE = HEAD_DIM ** (-0.5)
AHEAD = (2, 1)

VMEM = pl.BlockSpec(memory_space=pltpu.VMEM)
ANY = pl.BlockSpec(memory_space=pl.ANY)
HBM = pl.BlockSpec(memory_space=pltpu.HBM)
PARAMS = pltpu.CompilerParams(vmem_limit_bytes=16 * 1024 * 1024)


def shifted(array, axis, by):
    size = lax.axis_size(axis)
    return lax.ppermute(array, axis, [(i, (i + by) % size) for i in range(size)])


def is_power(n):
    return n & (n - 1) == 0


def partner(me, step, n, back=False):
    if is_power(n):
        return lax.bitwise_xor(me, step)
    return lax.rem(me + (n - step if back else step), n)


def exchange(array, axis, step):
    n = lax.axis_size(axis)
    if is_power(n):
        pairs = [(i, i ^ step) for i in range(n)]
    else:
        pairs = [(i, (i + step) % n) for i in range(n)]
    return lax.ppermute(array, axis, pairs)


def nt(a, b):
    return lax.dot_general(a, b, (((1,), (1,)), ((), ())), preferred_element_type=jnp.float32)


def nn(a, b):
    return lax.dot_general(a, b, (((1,), (0,)), ((), ())), preferred_element_type=jnp.float32)


def tn(a, b):
    return lax.dot_general(a, b, (((0,), (0,)), ((), ())), preferred_element_type=jnp.float32)


def prep_kernel(n, grad, key, value, *refs):
    slices, kv, sems = refs[:n], refs[n], refs[n + 1]
    me = lax.axis_index("uly")
    width = slices[0].shape[1]
    tokens = key.shape[0]
    copies = [
        pltpu.make_async_copy(key, kv.at[pl.ds(0, tokens)], sems.at[n]),
        pltpu.make_async_copy(value, kv.at[pl.ds(tokens, tokens)], sems.at[n + 1]),
    ]
    for step in range(n):
        to = partner(me, step, n) if step else me
        columns = pl.ds(pl.multiple_of(to * width, width), width)
        copies.append(pltpu.make_async_copy(grad.at[:, columns], slices[step], sems.at[step]))
    for copy in copies:
        copy.start()
    for copy in copies:
        copy.wait()


def turns(n):
    first = [0, n // 2] if n > 2 else [0]
    return first, [step for step in range(n - 1, 0, -1) if step not in first]


def ready(n):
    return [step for step in AHEAD if is_power(n) and step in turns(n)[0]]


def closing(n):
    return [n - 1] + list(range(1, n - 1))


def early_kernel(n, query, output, lse, kv, near_key, *refs):
    moved, refs = refs[: STEPS - 2], refs[STEPS - 2 :]
    keys, values, sides = refs[0], refs[1], refs[2:]
    me = lax.axis_index("uly")
    tokens = query.shape[0]
    rows = tokens // n
    kv_local = kv.shape[1] // HEAD_DIM
    for g in range(kv_local):
        cols = pl.ds(g * HEAD_DIM, HEAD_DIM)
        keys[g, pl.ds(0, tokens)] = kv[pl.ds(0, tokens), cols]
        values[g, pl.ds(0, tokens)] = kv[pl.ds(tokens, tokens), cols]
        keys[g, pl.ds(tokens, tokens)] = near_key[:, cols]
        for i in range(2, STEPS):
            part = pl.ds(i * tokens, tokens)
            keys[g, part] = moved[i - 2][pl.ds(0, tokens), cols]
            values[g, part] = moved[i - 2][pl.ds(tokens, tokens), cols]
    heads = kv_local * GROUP
    lanes = -(-tokens // 128) * 128
    lse_rows = jnp.concatenate([lse[...], jnp.zeros((-heads % 8, tokens), jnp.float32)], axis=0)
    if lanes > tokens:
        lse_rows = jnp.concatenate(
            [lse_rows, jnp.zeros((lse_rows.shape[0], lanes - tokens), jnp.float32)], axis=1
        )
    for half, steps in enumerate(turns(n)):
        prob, low, queries, outputs = sides[4 * half : 4 * half + 4]
        pieces = []
        for index, step in enumerate(steps):
            source = partner(me, step, n, back=True) if step else me
            start = pl.multiple_of(source * rows, rows)
            pieces.append(pltpu.roll(lse_rows, lax.rem(lanes - start, lanes), 1)[:, :rows])
            for g in range(kv_local):
                for h in range(GROUP):
                    head = pl.ds((g * GROUP + h) * HEAD_DIM, HEAD_DIM)
                    part = pl.ds((index * GROUP + h) * rows, rows)
                    queries[g, part] = query[pl.ds(start, rows), head]
                    outputs[g, part] = output[pl.ds(start, rows), head]
        for g in range(kv_local):
            lse_row = jnp.concatenate(
                [p[g * GROUP + h : g * GROUP + h + 1] for p in pieces for h in range(GROUP)], axis=1
            )
            wide = jnp.exp(nt(keys[g], queries[g]) * SCALE - lse_row)
            prob[g] = wide
            low[g] = wide.astype(jnp.bfloat16)


def halves_kernel(own, pair, first, second):
    rows = first.shape[0]
    odd = lax.rem(lax.axis_index("blk"), 2) == 1

    @pl.when(odd)
    def _():
        first[...] = pair[pl.ds(0, rows), :]
        second[...] = pair[pl.ds(rows, rows), :]

    @pl.when(jnp.logical_not(odd))
    def _():
        first[...] = own[pl.ds(0, rows), :]
        second[...] = own[pl.ds(rows, rows), :]


def score_grads(prob, outputs, values, pieces):
    heads = range(prob.shape[0])
    stacked, products = [], []
    for g in heads:
        go = jnp.concatenate(
            [
                piece[:, pl.ds((g * GROUP + h) * HEAD_DIM, HEAD_DIM)]
                for piece in pieces
                for h in range(GROUP)
            ],
            axis=0,
        )
        stacked.append(go)
        products.append(nt(values[g], go))
    deltas = [
        jnp.sum(stacked[g].astype(jnp.float32) * outputs[g].astype(jnp.float32), axis=1)[None, :]
        for g in heads
    ]
    scores = [
        (prob[g] * (products[g] - deltas[g])).astype(jnp.bfloat16) for g in heads
    ]
    return stacked, scores


def first_kernel(n, prob, low, queries, outputs, values, near_value, keys, *refs):
    steps = turns(n)[0]
    pieces, (joined, dq, dk, dv, *sends) = refs[: len(steps)], refs[len(steps) :]
    tokens = near_value.shape[0]
    near = pl.ds(tokens, tokens)
    for g in range(prob.shape[0]):
        joined[g] = values[g]
        joined[g, near] = near_value[:, pl.ds(g * HEAD_DIM, HEAD_DIM)]
    stacked, scores = score_grads(prob, outputs, joined, pieces)
    rows = pieces[0].shape[0]
    for g in range(prob.shape[0]):
        dk[g] = nn(scores[g], queries[g])
        dv[g] = nn(low[g], stacked[g])
        query_rows = (tn(scores[g], keys[g]) * SCALE).astype(jnp.bfloat16)
        for index in range(len(pieces)):
            for h in range(GROUP):
                start = (index * GROUP + h) * rows
                dq[pl.ds(index * rows, rows), pl.ds((g * GROUP + h) * HEAD_DIM, HEAD_DIM)] = (
                    query_rows[start : start + rows]
                )
    for step, send in zip(ready(n), sends):
        send[...] = dq[pl.ds(steps.index(step) * rows, rows), :]


def main_kernel(prob, low, queries, outputs, values, dk_first, dv_first, *refs):
    pieces, (*far, own, dscore) = refs[: -STEPS - 1], refs[-STEPS - 1 :]
    tokens = values.shape[1] // STEPS
    stacked, scores = score_grads(prob, outputs, values, pieces)
    for g in range(prob.shape[0]):
        cols = pl.ds(g * HEAD_DIM, HEAD_DIM)
        dscore[g] = scores[g]
        dk = (nn(scores[g], queries[g]) + dk_first[g]) * SCALE
        dv = nn(low[g], stacked[g]) + dv_first[g]
        own[pl.ds(0, tokens), cols] = dk[:tokens]
        own[pl.ds(tokens, tokens), cols] = dv[:tokens]
        for i in range(1, STEPS):
            part = slice(i * tokens, (i + 1) * tokens)
            far[i - 1][pl.ds(0, tokens), cols] = dk[part].astype(jnp.bfloat16)
            far[i - 1][pl.ds(tokens, tokens), cols] = dv[part].astype(jnp.bfloat16)


def query_kernel(n, keys, dq_first, dscore, out, *sends):
    rows = out.shape[0] // n
    me = lax.axis_index("uly")
    first, last = turns(n)
    for index, step in enumerate(first):
        source = partner(me, step, n, back=True) if step else me
        out[pl.ds(pl.multiple_of(source * rows, rows), rows), :] = dq_first[
            pl.ds(index * rows, rows), :
        ]
    for g in range(keys.shape[0]):
        dq = (tn(dscore[g], keys[g]) * SCALE).astype(jnp.bfloat16)
        for index, step in enumerate(last):
            start = pl.multiple_of(partner(me, step, n, back=True) * rows, rows)
            for h in range(GROUP):
                at = (index * GROUP + h) * rows
                out[pl.ds(start, rows), pl.ds((g * GROUP + h) * HEAD_DIM, HEAD_DIM)] = dq[
                    at : at + rows
                ]
    for step, send in zip([step for step in AHEAD if step not in ready(n)], sends):
        start = pl.multiple_of(partner(me, step, n) * rows, rows)
        send[...] = out[pl.ds(start, rows), :]


def sum_kernel(n, dq, own, *refs):
    back = refs[: STEPS - 1]
    sends, total = refs[STEPS - 1 : -1], refs[-1]
    me = lax.axis_index("uly")
    width = dq.shape[1]
    kv_width = own.shape[1]
    tokens = dq.shape[0]
    rows = tokens // n
    acc = own[...]
    for b in back:
        acc = acc + b[...].astype(jnp.float32)
    total[...] = acc.astype(jnp.bfloat16)
    for step in range(n):
        to = partner(me, step, n) if step else me
        start = pl.multiple_of(to * rows, rows)
        first = 0 if step in AHEAD else width
        if first:
            sends[step][:, pl.ds(0, width)] = dq[pl.ds(start, rows), :]
        sends[step][:, pl.ds(first, kv_width)] = total[pl.ds(start, rows), :]
        sends[step][:, pl.ds(first + kv_width, kv_width)] = total[
            pl.ds(pl.multiple_of(start + tokens, rows), rows), :
        ]


def stash_kernel(*refs):
    half = len(refs) // 2
    for source, target in zip(refs[:half], refs[half:]):
        target[...] = source[...]


def place_kernel(n, *refs):
    parts, refs = dict(zip(closing(n) + [0], refs[:n])), refs[n:]
    ahead, (dq, dk, dv, sems) = refs[: len(AHEAD)], refs[len(AHEAD) :]
    me = lax.axis_index("uly")
    width = dq.shape[1] // n
    kv_width = dk.shape[1] // n
    copies = []
    for step in range(n):
        source = partner(me, step, n, back=True) if step else me
        first = 0 if step in AHEAD else width
        pieces = (
            (dk, parts[step], first, kv_width),
            (dv, parts[step], first + kv_width, kv_width),
            (dq, ahead[AHEAD.index(step)] if step in AHEAD else parts[step], 0, width),
        )
        for i, (out, part, at, size) in enumerate(pieces):
            columns = pl.ds(pl.multiple_of(source * size, size), size)
            copies.append(
                pltpu.make_async_copy(
                    part.at[:, pl.ds(at, size)], out.at[:, columns], sems.at[step, i]
                )
            )
    for copy in copies:
        copy.start()
    for copy in copies:
        copy.wait()


def shape(dims, kind=jnp.bfloat16):
    return jax.ShapeDtypeStruct(dims, kind)


def body(query, key, value, output, grad, lse):
    n = lax.axis_size("uly")
    tokens, width = query.shape
    kv_width = key.shape[1]
    kv_local = kv_width // HEAD_DIM
    rows = grad.shape[0]
    key_rows, query_rows = STEPS * tokens, GROUP * tokens
    far_grad, far_key, far_value = (
        pltpu.with_memory_space_constraint(a, pltpu.HBM) for a in (grad, key, value)
    )
    *slices, kv = pl.pallas_call(
        functools.partial(prep_kernel, n),
        out_shape=[shape((rows, width))] * n + [shape((2 * tokens, kv_width))],
        in_specs=[HBM] * 3,
        out_specs=[ANY] * (n + 1),
        scratch_shapes=[pltpu.SemaphoreType.DMA((n + 2,))],
        compiler_params=PARAMS,
        name="prep",
    )(far_grad, far_key, far_value)
    received = [exchange(slices[step], "uly", step) for step in range(1, n)]
    moved = [shifted(kv, "blk", i) for i in range(2, STEPS)]
    swap = [(i, i ^ 1) for i in range(lax.axis_size("blk"))]
    passed = pl.pallas_call(
        halves_kernel,
        out_shape=[shape((tokens, kv_width))] * 2,
        in_specs=[VMEM] * 2,
        out_specs=[VMEM] * 2,
        compiler_params=PARAMS,
        cost_estimate=pl.CostEstimate(flops=1000000000, bytes_accessed=1000, transcendentals=0),
        name="halves",
    )(kv, moved[0])
    near_key, near_value = [lax.ppermute(a, "blk", swap) for a in passed]
    columns = [len(steps) * GROUP * rows for steps in turns(n)]
    keys, values, *sides = pl.pallas_call(
        functools.partial(early_kernel, n),
        out_shape=[shape((kv_local, key_rows, HEAD_DIM))] * 2
        + [
            shape(*dims)
            for c in columns
            for dims in (
                ((kv_local, key_rows, c), jnp.float32),
                ((kv_local, key_rows, c),),
                ((kv_local, c, HEAD_DIM),),
                ((kv_local, c, HEAD_DIM),),
            )
        ],
        in_specs=[VMEM] * (3 + STEPS),
        out_specs=[VMEM] * 10,
        compiler_params=PARAMS,
        name="early",
    )(query, output, lse, kv, near_key, *moved)
    received = [slices[0]] + received
    first, last = ([received[step] for step in steps] for steps in turns(n))
    part = shape((kv_local, key_rows, HEAD_DIM), jnp.float32)
    joined, dq_first, *parts_first = pl.pallas_call(
        functools.partial(first_kernel, n),
        out_shape=[shape(values.shape), shape((len(first) * rows, width)), part, part]
        + [shape((rows, width))] * len(ready(n)),
        in_specs=[VMEM] * (7 + len(first)),
        out_specs=[VMEM] * (4 + len(ready(n))),
        compiler_params=PARAMS,
        name="first",
    )(*sides[:4], values, near_value, keys, *first)
    *far, own, dscore = pl.pallas_call(
        main_kernel,
        out_shape=[shape((2 * tokens, kv_width))] * (STEPS - 1)
        + [
            shape((2 * tokens, kv_width), jnp.float32),
            shape((kv_local, key_rows, columns[1])),
        ],
        in_specs=[VMEM] * (7 + len(last)),
        out_specs=[VMEM] * (STEPS + 1),
        compiler_params=PARAMS,
        name="main",
    )(*sides[4:], joined, *parts_first[:2], *last)
    back = [shifted(far[i - 1], "blk", -i) for i in range(STEPS - 1, 0, -1)]
    dq, *ahead = pl.pallas_call(
        functools.partial(query_kernel, n),
        out_shape=[shape((tokens, width))] + [shape((rows, width))] * (len(AHEAD) - len(ready(n))),
        in_specs=[VMEM] * 3,
        out_specs=[VMEM] * (1 + len(AHEAD) - len(ready(n))),
        compiler_params=PARAMS,
        name="query",
    )(keys, dq_first, dscore)
    early_sends, later_sends = iter(parts_first[2:]), iter(ahead)
    ahead = [
        exchange(next(early_sends if step in ready(n) else later_sends), "uly", step)
        for step in AHEAD
    ]
    *parts, = pl.pallas_call(
        functools.partial(sum_kernel, n),
        out_shape=[
            shape((rows, 2 * kv_width + (0 if step in AHEAD else width))) for step in range(n)
        ],
        in_specs=[VMEM] * (STEPS + 1),
        out_specs=[VMEM] * n,
        scratch_shapes=[pltpu.VMEM((2 * tokens, kv_width), jnp.bfloat16)],
        compiler_params=PARAMS,
        name="sum",
    )(dq, own, *back)
    final = [parts[0]] + [exchange(parts[step], "uly", step) for step in range(1, n)]
    ahead = pl.pallas_call(
        stash_kernel,
        out_shape=[shape((rows, width))] * len(AHEAD),
        in_specs=[VMEM] * len(AHEAD),
        out_specs=[VMEM] * len(AHEAD),
        compiler_params=PARAMS,
        cost_estimate=pl.CostEstimate(flops=300 * 10**6, bytes_accessed=1000, transcendentals=0),
        name="stash",
    )(*ahead)
    return pl.pallas_call(
        functools.partial(place_kernel, n),
        out_shape=[
            shape((rows, width * n)),
            shape((rows, kv_width * n)),
            shape((rows, kv_width * n)),
        ],
        in_specs=[ANY] * (n + len(AHEAD)),
        out_specs=[HBM] * 3,
        scratch_shapes=[pltpu.SemaphoreType.DMA((n, 3))],
        compiler_params=PARAMS,
        name="place",
    )(*(final[step] for step in closing(n)), final[0], *ahead)


def solution(mesh):
    placed = (
        P("blk", "uly"),
        P("blk", "uly"),
        P("blk", "uly"),
        P("blk", "uly"),
        P(("blk", "uly"), None),
        P("uly", "blk"),
    )
    return jax.shard_map(
        lambda *args: tuple(body(*args)),
        mesh=mesh,
        in_specs=placed,
        out_specs=(P(("blk", "uly"), None), P(("blk", "uly"), None), P(("blk", "uly"), None)),
        check_vma=False,
    )
```

```python
import functools

import jax
import jax.numpy as jnp
from jax import lax
from jax.experimental import pallas as pl
from jax.experimental.pallas import tpu as pltpu
from jax.sharding import PartitionSpec as P

QHEADS = 40
KVHEADS = 8
HEAD_DIM = 128
STEPS = 3
GROUP = QHEADS // KVHEADS
SCALE = HEAD_DIM ** (-0.5)
AHEAD = (1, 2)

VMEM = pl.BlockSpec(memory_space=pltpu.VMEM)
ANY = pl.BlockSpec(memory_space=pl.ANY)
HBM = pl.BlockSpec(memory_space=pltpu.HBM)
PARAMS = pltpu.CompilerParams(vmem_limit_bytes=16 * 1024 * 1024)


def shifted(array, axis, by):
    size = lax.axis_size(axis)
    return lax.ppermute(array, axis, [(i, (i + by) % size) for i in range(size)])


def is_power(n):
    return n & (n - 1) == 0


def partner(me, step, n, back=False):
    if is_power(n):
        return lax.bitwise_xor(me, step)
    return lax.rem(me + (n - step if back else step), n)


def exchange(array, axis, step):
    n = lax.axis_size(axis)
    if is_power(n):
        pairs = [(i, i ^ step) for i in range(n)]
    else:
        pairs = [(i, (i + step) % n) for i in range(n)]
    return lax.ppermute(array, axis, pairs)


def nt(a, b):
    return lax.dot_general(a, b, (((1,), (1,)), ((), ())), preferred_element_type=jnp.float32)


def nn(a, b):
    return lax.dot_general(a, b, (((1,), (0,)), ((), ())), preferred_element_type=jnp.float32)


def tn(a, b):
    return lax.dot_general(a, b, (((0,), (0,)), ((), ())), preferred_element_type=jnp.float32)


def prep_kernel(n, grad, key, value, *refs):
    slices, kv, sems = refs[:n], refs[n], refs[n + 1]
    me = lax.axis_index("uly")
    width = slices[0].shape[1]
    tokens = key.shape[0]
    copies = [
        pltpu.make_async_copy(key, kv.at[pl.ds(0, tokens)], sems.at[n]),
        pltpu.make_async_copy(value, kv.at[pl.ds(tokens, tokens)], sems.at[n + 1]),
    ]
    for step in range(n):
        to = partner(me, step, n) if step else me
        columns = pl.ds(pl.multiple_of(to * width, width), width)
        copies.append(pltpu.make_async_copy(grad.at[:, columns], slices[step], sems.at[step]))
    for copy in copies:
        copy.start()
    for copy in copies:
        copy.wait()


def turns(n):
    first = [0, n // 2] if n > 2 else [0]
    return first, [step for step in range(n - 1, 0, -1) if step not in first]


def ready(n):
    return [step for step in AHEAD if is_power(n) and step in turns(n)[0]]


def closing(n):
    return [n - 1] + list(range(1, n - 1))


def early_kernel(n, query, output, lse, kv, near_key, *refs):
    moved, refs = refs[: STEPS - 2], refs[STEPS - 2 :]
    keys, values, sides = refs[0], refs[1], refs[2:]
    me = lax.axis_index("uly")
    tokens = query.shape[0]
    rows = tokens // n
    kv_local = kv.shape[1] // HEAD_DIM
    for g in range(kv_local):
        cols = pl.ds(g * HEAD_DIM, HEAD_DIM)
        keys[g, pl.ds(0, tokens)] = kv[pl.ds(0, tokens), cols]
        values[g, pl.ds(0, tokens)] = kv[pl.ds(tokens, tokens), cols]
        keys[g, pl.ds(tokens, tokens)] = near_key[:, cols]
        for i in range(2, STEPS):
            part = pl.ds(i * tokens, tokens)
            keys[g, part] = moved[i - 2][pl.ds(0, tokens), cols]
            values[g, part] = moved[i - 2][pl.ds(tokens, tokens), cols]
    heads = kv_local * GROUP
    lanes = -(-tokens // 128) * 128
    lse_rows = jnp.concatenate([lse[...], jnp.zeros((-heads % 8, tokens), jnp.float32)], axis=0)
    if lanes > tokens:
        lse_rows = jnp.concatenate(
            [lse_rows, jnp.zeros((lse_rows.shape[0], lanes - tokens), jnp.float32)], axis=1
        )
    for half, steps in enumerate(turns(n)):
        prob, low, queries, outputs = sides[4 * half : 4 * half + 4]
        pieces = []
        for index, step in enumerate(steps):
            source = partner(me, step, n, back=True) if step else me
            start = pl.multiple_of(source * rows, rows)
            pieces.append(pltpu.roll(lse_rows, lax.rem(lanes - start, lanes), 1)[:, :rows])
            for g in range(kv_local):
                for h in range(GROUP):
                    head = pl.ds((g * GROUP + h) * HEAD_DIM, HEAD_DIM)
                    part = pl.ds((index * GROUP + h) * rows, rows)
                    queries[g, part] = query[pl.ds(start, rows), head]
                    outputs[g, part] = output[pl.ds(start, rows), head]
        for g in range(kv_local):
            lse_row = jnp.concatenate(
                [p[g * GROUP + h : g * GROUP + h + 1] for p in pieces for h in range(GROUP)], axis=1
            )
            wide = jnp.exp(nt(keys[g], queries[g]) * SCALE - lse_row)
            prob[g] = wide
            low[g] = wide.astype(jnp.bfloat16)


def halves_kernel(own, pair, first, second):
    rows = first.shape[0]
    odd = lax.rem(lax.axis_index("blk"), 2) == 1

    @pl.when(odd)
    def _():
        first[...] = pair[pl.ds(0, rows), :]
        second[...] = pair[pl.ds(rows, rows), :]

    @pl.when(jnp.logical_not(odd))
    def _():
        first[...] = own[pl.ds(0, rows), :]
        second[...] = own[pl.ds(rows, rows), :]


def score_grads(prob, outputs, values, near_value, pieces):
    tokens = near_value.shape[0]
    heads = range(prob.shape[0])
    stacked, products = [], []
    for g in heads:
        v = jnp.concatenate(
            [
                values[g, pl.ds(0, tokens)],
                near_value[:, pl.ds(g * HEAD_DIM, HEAD_DIM)],
                values[g, pl.ds(2 * tokens, (STEPS - 2) * tokens)],
            ],
            axis=0,
        )
        go = jnp.concatenate(
            [
                piece[:, pl.ds((g * GROUP + h) * HEAD_DIM, HEAD_DIM)]
                for piece in pieces
                for h in range(GROUP)
            ],
            axis=0,
        )
        stacked.append(go)
        products.append(nt(v, go))
    deltas = [
        jnp.sum(stacked[g].astype(jnp.float32) * outputs[g].astype(jnp.float32), axis=1)[None, :]
        for g in heads
    ]
    scores = [
        (prob[g] * (products[g] - deltas[g])).astype(jnp.bfloat16) for g in heads
    ]
    return stacked, scores


def first_kernel(n, prob, low, queries, outputs, values, near_value, keys, *refs):
    steps = turns(n)[0]
    pieces, (dq, dk, dv, *sends) = refs[: len(steps)], refs[len(steps) :]
    stacked, scores = score_grads(prob, outputs, values, near_value, pieces)
    rows = pieces[0].shape[0]
    for g in range(prob.shape[0]):
        dk[g] = nn(scores[g], queries[g])
        dv[g] = nn(low[g], stacked[g])
        query_rows = (tn(scores[g], keys[g]) * SCALE).astype(jnp.bfloat16)
        for index in range(len(pieces)):
            for h in range(GROUP):
                start = (index * GROUP + h) * rows
                dq[pl.ds(index * rows, rows), pl.ds((g * GROUP + h) * HEAD_DIM, HEAD_DIM)] = (
                    query_rows[start : start + rows]
                )
    for step, send in zip(ready(n), sends):
        send[...] = dq[pl.ds(steps.index(step) * rows, rows), :]


def main_kernel(prob, low, queries, outputs, values, near_value, dk_first, dv_first, *refs):
    pieces, (*far, own, dscore) = refs[: -STEPS - 1], refs[-STEPS - 1 :]
    tokens = near_value.shape[0]
    stacked, scores = score_grads(prob, outputs, values, near_value, pieces)
    for g in range(prob.shape[0]):
        cols = pl.ds(g * HEAD_DIM, HEAD_DIM)
        dscore[g] = scores[g]
        dk = (nn(scores[g], queries[g]) + dk_first[g]) * SCALE
        dv = nn(low[g], stacked[g]) + dv_first[g]
        own[pl.ds(0, tokens), cols] = dk[:tokens]
        own[pl.ds(tokens, tokens), cols] = dv[:tokens]
        for i in range(1, STEPS):
            part = slice(i * tokens, (i + 1) * tokens)
            far[i - 1][pl.ds(0, tokens), cols] = dk[part].astype(jnp.bfloat16)
            far[i - 1][pl.ds(tokens, tokens), cols] = dv[part].astype(jnp.bfloat16)


def query_kernel(n, keys, dq_first, dscore, out, *sends):
    rows = out.shape[0] // n
    me = lax.axis_index("uly")
    first, last = turns(n)
    for index, step in enumerate(first):
        source = partner(me, step, n, back=True) if step else me
        out[pl.ds(pl.multiple_of(source * rows, rows), rows), :] = dq_first[
            pl.ds(index * rows, rows), :
        ]
    for g in range(keys.shape[0]):
        dq = (tn(dscore[g], keys[g]) * SCALE).astype(jnp.bfloat16)
        for index, step in enumerate(last):
            start = pl.multiple_of(partner(me, step, n, back=True) * rows, rows)
            for h in range(GROUP):
                at = (index * GROUP + h) * rows
                out[pl.ds(start, rows), pl.ds((g * GROUP + h) * HEAD_DIM, HEAD_DIM)] = dq[
                    at : at + rows
                ]
    for step, send in zip([step for step in AHEAD if step not in ready(n)], sends):
        start = pl.multiple_of(partner(me, step, n) * rows, rows)
        send[...] = out[pl.ds(start, rows), :]


def sum_kernel(n, dq, own, *refs):
    back = refs[: STEPS - 1]
    sends, total = refs[STEPS - 1 : -1], refs[-1]
    me = lax.axis_index("uly")
    width = dq.shape[1]
    kv_width = own.shape[1]
    tokens = dq.shape[0]
    rows = tokens // n
    acc = own[...]
    for b in back:
        acc = acc + b[...].astype(jnp.float32)
    total[...] = acc.astype(jnp.bfloat16)
    for step in range(n):
        to = partner(me, step, n) if step else me
        start = pl.multiple_of(to * rows, rows)
        first = 0 if step in AHEAD else width
        if first:
            sends[step][:, pl.ds(0, width)] = dq[pl.ds(start, rows), :]
        sends[step][:, pl.ds(first, kv_width)] = total[pl.ds(start, rows), :]
        sends[step][:, pl.ds(first + kv_width, kv_width)] = total[
            pl.ds(pl.multiple_of(start + tokens, rows), rows), :
        ]


def stash_kernel(*refs):
    half = len(refs) // 2
    for source, target in zip(refs[:half], refs[half:]):
        target[...] = source[...]


def place_kernel(n, *refs):
    parts, refs = dict(zip(closing(n) + [0], refs[:n])), refs[n:]
    ahead, (dq, dk, dv, sems) = refs[: len(AHEAD)], refs[len(AHEAD) :]
    me = lax.axis_index("uly")
    width = dq.shape[1] // n
    kv_width = dk.shape[1] // n
    copies = []
    for step in range(n):
        source = partner(me, step, n, back=True) if step else me
        first = 0 if step in AHEAD else width
        pieces = (
            (dk, parts[step], first, kv_width),
            (dv, parts[step], first + kv_width, kv_width),
            (dq, ahead[AHEAD.index(step)] if step in AHEAD else parts[step], 0, width),
        )
        for i, (out, part, at, size) in enumerate(pieces):
            columns = pl.ds(pl.multiple_of(source * size, size), size)
            copies.append(
                pltpu.make_async_copy(
                    part.at[:, pl.ds(at, size)], out.at[:, columns], sems.at[step, i]
                )
            )
    for copy in copies:
        copy.start()
    for copy in copies:
        copy.wait()


def shape(dims, kind=jnp.bfloat16):
    return jax.ShapeDtypeStruct(dims, kind)


def body(query, key, value, output, grad, lse):
    n = lax.axis_size("uly")
    tokens, width = query.shape
    kv_width = key.shape[1]
    kv_local = kv_width // HEAD_DIM
    rows = grad.shape[0]
    key_rows, query_rows = STEPS * tokens, GROUP * tokens
    far_grad, far_key, far_value = (
        pltpu.with_memory_space_constraint(a, pltpu.HBM) for a in (grad, key, value)
    )
    *slices, kv = pl.pallas_call(
        functools.partial(prep_kernel, n),
        out_shape=[shape((rows, width))] * n + [shape((2 * tokens, kv_width))],
        in_specs=[HBM] * 3,
        out_specs=[ANY] * (n + 1),
        scratch_shapes=[pltpu.SemaphoreType.DMA((n + 2,))],
        compiler_params=PARAMS,
        name="prep",
    )(far_grad, far_key, far_value)
    received = [exchange(slices[step], "uly", step) for step in range(1, n)]
    moved = [shifted(kv, "blk", i) for i in range(2, STEPS)]
    swap = [(i, i ^ 1) for i in range(lax.axis_size("blk"))]
    passed = pl.pallas_call(
        halves_kernel,
        out_shape=[shape((tokens, kv_width))] * 2,
        in_specs=[VMEM] * 2,
        out_specs=[VMEM] * 2,
        compiler_params=PARAMS,
        cost_estimate=pl.CostEstimate(flops=1000000000, bytes_accessed=1000, transcendentals=0),
        name="halves",
    )(kv, moved[0])
    near_key, near_value = [lax.ppermute(a, "blk", swap) for a in passed]
    columns = [len(steps) * GROUP * rows for steps in turns(n)]
    keys, values, *sides = pl.pallas_call(
        functools.partial(early_kernel, n),
        out_shape=[shape((kv_local, key_rows, HEAD_DIM))] * 2
        + [
            shape(*dims)
            for c in columns
            for dims in (
                ((kv_local, key_rows, c), jnp.float32),
                ((kv_local, key_rows, c),),
                ((kv_local, c, HEAD_DIM),),
                ((kv_local, c, HEAD_DIM),),
            )
        ],
        in_specs=[VMEM] * (3 + STEPS),
        out_specs=[VMEM] * 10,
        compiler_params=PARAMS,
        name="early",
    )(query, output, lse, kv, near_key, *moved)
    received = [slices[0]] + received
    first, last = ([received[step] for step in steps] for steps in turns(n))
    part = shape((kv_local, key_rows, HEAD_DIM), jnp.float32)
    dq_first, *parts_first = pl.pallas_call(
        functools.partial(first_kernel, n),
        out_shape=[shape((len(first) * rows, width)), part, part]
        + [shape((rows, width))] * len(ready(n)),
        in_specs=[VMEM] * (7 + len(first)),
        out_specs=[VMEM] * (3 + len(ready(n))),
        compiler_params=PARAMS,
        name="first",
    )(*sides[:4], values, near_value, keys, *first)
    *far, own, dscore = pl.pallas_call(
        main_kernel,
        out_shape=[shape((2 * tokens, kv_width))] * (STEPS - 1)
        + [
            shape((2 * tokens, kv_width), jnp.float32),
            shape((kv_local, key_rows, columns[1])),
        ],
        in_specs=[VMEM] * (8 + len(last)),
        out_specs=[VMEM] * (STEPS + 1),
        compiler_params=PARAMS,
        name="main",
    )(*sides[4:], values, near_value, *parts_first[:2], *last)
    back = [shifted(far[i - 1], "blk", -i) for i in range(STEPS - 1, 0, -1)]
    dq, *ahead = pl.pallas_call(
        functools.partial(query_kernel, n),
        out_shape=[shape((tokens, width))] + [shape((rows, width))] * (len(AHEAD) - len(ready(n))),
        in_specs=[VMEM] * 3,
        out_specs=[VMEM] * (1 + len(AHEAD) - len(ready(n))),
        compiler_params=PARAMS,
        name="query",
    )(keys, dq_first, dscore)
    early_sends, later_sends = iter(parts_first[2:]), iter(ahead)
    ahead = [
        exchange(next(early_sends if step in ready(n) else later_sends), "uly", step)
        for step in AHEAD
    ]
    *parts, = pl.pallas_call(
        functools.partial(sum_kernel, n),
        out_shape=[
            shape((rows, 2 * kv_width + (0 if step in AHEAD else width))) for step in range(n)
        ],
        in_specs=[VMEM] * (STEPS + 1),
        out_specs=[VMEM] * n,
        scratch_shapes=[pltpu.VMEM((2 * tokens, kv_width), jnp.bfloat16)],
        compiler_params=PARAMS,
        name="sum",
    )(dq, own, *back)
    final = [parts[0]] + [exchange(parts[step], "uly", step) for step in range(1, n)]
    ahead = pl.pallas_call(
        stash_kernel,
        out_shape=[shape((rows, width))] * len(AHEAD),
        in_specs=[VMEM] * len(AHEAD),
        out_specs=[VMEM] * len(AHEAD),
        compiler_params=PARAMS,
        cost_estimate=pl.CostEstimate(flops=300 * 10**6, bytes_accessed=1000, transcendentals=0),
        name="stash",
    )(*ahead)
    return pl.pallas_call(
        functools.partial(place_kernel, n),
        out_shape=[
            shape((rows, width * n)),
            shape((rows, kv_width * n)),
            shape((rows, kv_width * n)),
        ],
        in_specs=[ANY] * (n + len(AHEAD)),
        out_specs=[HBM] * 3,
        scratch_shapes=[pltpu.SemaphoreType.DMA((n, 3))],
        compiler_params=PARAMS,
        name="place",
    )(*(final[step] for step in closing(n)), final[0], *ahead)


def solution(mesh):
    placed = (
        P("blk", "uly"),
        P("blk", "uly"),
        P("blk", "uly"),
        P("blk", "uly"),
        P(("blk", "uly"), None),
        P("uly", "blk"),
    )
    return jax.shard_map(
        lambda *args: tuple(body(*args)),
        mesh=mesh,
        in_specs=placed,
        out_specs=(P(("blk", "uly"), None), P(("blk", "uly"), None), P(("blk", "uly"), None)),
        check_vma=False,
    )
```
